128 devices in a mesh: blk: 16 (over z, y), pair: 8 (over x, core).
Axes of the slice: x: 4, y: 4, z: 4, core: 2. Of those that a mesh axis runs over, the one named last changes fastest.
Arguments:
- amplitudes: bfloat16 [128, 524288], P('pair', 'blk'), may hold values from -6 to 6
- integrals: bfloat16 [10240, 4, 128, 128], P(('blk', 'pair')), may hold values from -0.25 to 0.25
- block_irrep: int32 [4096], replicated, may hold values from 0 to 7
- slab_blocks: int32 [32], replicated, may hold values from 0 to 4095, as said below
- owner: int32 [4096], replicated, may hold values from 0 to 127, as said below
- partner: int32 [4096], replicated, may hold values from 0 to 4095, as said below
- sign: int32 [4096], replicated, may hold values from -1 to 1, as said below
Outputs:
- ladder: bfloat16 [128, 524288], P('pair', 'blk')
The draws below stay inside these ranges and needn't reach their ends.
Inputs may be any that keep to these rules, and one draw needn't show every extreme that they name: Distinct blocks; block_irrep[slab_blocks[g * 4 + k]] = g. `owner`: flat device index (blk index times the pair axis's size plus pair index). For each blk index t, of the blocks t * 256 to t * 256 + 255 exactly 256 divided by the pair axis's size are stored on each pair index, at most 5 on any one device, and some device stores exactly 5 of them for every t. Integral rows not named by any block are read by no output. An involution without fixed points; for any blk indices t and t2, equal or not, exactly 256 divided by the blk axis's size of the blocks of t have their partner among the blocks of t2. `sign`: each entry is -1 or 1.
All inputs are finite; a program needn't handle non-finite values.
Results may differ from the reference program's by a relative error of at most 0.001.
Values may be sent and summed in bfloat16 or wider, within the bound.
No kernel may reach another device: no remote copies, remote signals or barrier semaphores. Data moves between devices by JAX's collectives and lax.ppermute only.
A program may use at most 128 MiB of HBM per device.

```python
import jax
import jax.numpy as jnp
from jax import lax

W = 128
IRREPS = 8
CPI = 4
BLK_DEV = 256
NB = 4096
PAIRS = 128
CAP = 5
SLOTS = 80
N_BLK = 16
N_PAIR = 8
DEVICES = 128


def irrep_layout(key):
    base = jax.random.fold_in(key, 7)
    shuffled = jax.random.permutation(jax.random.fold_in(base, 1), NB)
    others = jax.random.randint(jax.random.fold_in(base, 2), (NB,), 0, IRREPS)
    position_ids = jnp.arange(NB)
    label_at = jnp.where(position_ids < IRREPS * CPI, position_ids // CPI, others).astype(jnp.int32)
    labels = jnp.zeros((NB,), jnp.int32).at[shuffled].set(label_at)
    chosen = shuffled[:IRREPS * CPI].astype(jnp.int32)
    return (labels, chosen)


def draw_block_irrep(key, part):
    labels, chosen = irrep_layout(key)
    return labels


def draw_slab_blocks(key, part):
    labels, chosen = irrep_layout(key)
    return chosen


def draw_owner(key, part):
    base = jax.random.fold_in(key, 11)
    heavy_order = jax.random.permutation(jax.random.fold_in(base, 1), N_BLK)
    range_keys = jax.random.split(jax.random.fold_in(base, 2), N_BLK)
    shuffles = jax.vmap(lambda one_key: jax.random.permutation(one_key, BLK_DEV))(range_keys)
    local_ids = jnp.arange(BLK_DEV)
    group_len = BLK_DEV // N_PAIR
    stored_pair = local_ids // group_len
    within = local_ids % group_len
    light_count = BLK_DEV // (2 * DEVICES)
    heavy_total = 5 * light_count * (N_BLK // 4)
    place = jnp.where(within < heavy_total, within // (5 * light_count), N_BLK // 4 + (within - heavy_total) // light_count)
    stored_blk = heavy_order[place]
    flat_device = (stored_blk * N_PAIR + stored_pair).astype(jnp.int32)
    range_rows = jnp.broadcast_to(jnp.arange(N_BLK)[:, None], (N_BLK, BLK_DEV))
    grid = jnp.zeros((N_BLK, BLK_DEV), jnp.int32).at[range_rows, shuffles].set(jnp.broadcast_to(flat_device[None, :], (N_BLK, BLK_DEV)))
    return grid.reshape(NB)


def draw_partner(key, part):
    base = jax.random.fold_in(key, 13)
    range_keys = jax.random.split(base, N_BLK)
    shuffles = jax.vmap(lambda one_key: jax.random.permutation(one_key, BLK_DEV))(range_keys)
    group_len = BLK_DEV // N_BLK
    block_grid = (jnp.arange(N_BLK)[:, None] * BLK_DEV + shuffles).astype(jnp.int32).reshape(N_BLK, N_BLK, group_len)
    mates = jnp.swapaxes(block_grid, 0, 1)
    rolled = jnp.roll(block_grid, group_len // 2, axis=2)
    diagonal = (jnp.arange(N_BLK)[:, None] == jnp.arange(N_BLK)[None, :])[:, :, None]
    mates = jnp.where(diagonal, rolled, mates)
    return jnp.zeros((NB,), jnp.int32).at[block_grid.reshape(-1)].set(mates.reshape(-1))


def draw_sign(key, part):
    coins = jax.random.randint(jax.random.fold_in(key, 17), (NB,), 0, 2)
    return (2 * coins - 1).astype(jnp.int32)


def shard_levels(stream_key, shape, cuts, least, largest):
    loudness = 1.0
    for position, shards_of in cuts:
        draws = jax.random.uniform(jax.random.fold_in(jax.random.fold_in(stream_key, 6), position), (shards_of,), jnp.float32, least / len(cuts), largest / len(cuts))
        loudness = loudness * jnp.repeat(jnp.exp(draws), shape[position] // shards_of).reshape((-1,) + (1,) * (len(shape) - 1 - position))
    return loudness


def centred(key, extent, scale, limit, shards=(), held_as=jnp.bfloat16):
    factor_of = shard_levels(key, extent, shards, -0.22, 0.18) if shards else 1.0
    drawn = jax.random.normal(key, extent, jnp.float32) * scale * factor_of
    return jnp.minimum(jnp.maximum(drawn, -limit), limit).astype(held_as)


def setup_inputs(seed: int = 0) -> dict:
    keys = jax.random.split(jax.random.key(seed), 8)
    amplitudes = centred(keys[0], (PAIRS, NB * W), 1.0, 6.0, ((0, 8), (1, 16)))
    integrals = centred(keys[1], (DEVICES * SLOTS, CPI, W, W), (CPI * W) ** -0.5, 0.25, ((0, 128),))
    block_irrep = draw_block_irrep(jax.random.fold_in(keys[7], 71), 0)
    slab_blocks = draw_slab_blocks(jax.random.fold_in(keys[7], 71), 0)
    owner = draw_owner(jax.random.fold_in(keys[7], 71), 0)
    partner = draw_partner(jax.random.fold_in(keys[7], 71), 0)
    sign = draw_sign(jax.random.fold_in(keys[7], 71), 0)
    return {"amplitudes": amplitudes, "integrals": integrals, "block_irrep": block_irrep, "slab_blocks": slab_blocks, "owner": owner, "partner": partner, "sign": sign}


def earlier_matches(labels):
    span_length = labels.shape[1]
    position_ids = jnp.arange(span_length, dtype=jnp.int32)
    earlier_mask = position_ids[None, :] < position_ids[:, None]
    same_label = labels[:, :, None] == labels[:, None, :]
    return jnp.sum(jnp.logical_and(same_label, earlier_mask[None]), axis=2).astype(jnp.int32)


def reference(amplitudes, integrals, block_irrep, slab_blocks, owner, partner, sign):
    block_ids = jnp.arange(NB, dtype=jnp.int32)
    block_ranks = earlier_matches(owner.reshape(N_BLK, BLK_DEV)).reshape(NB)
    tile_rows = (owner * SLOTS + (block_ids // BLK_DEV) * CAP + block_ranks).astype(jnp.int32)
    amp_blocks = amplitudes.reshape(PAIRS, NB, W)
    slab_matrix = jnp.take(amp_blocks, slab_blocks, axis=1).reshape(PAIRS, IRREPS, CPI * W)
    batch_size = BLK_DEV // 4

    def one_batch(chosen):
        tile_batch = jnp.take(integrals, jnp.take(tile_rows, chosen), axis=0).reshape(batch_size, CPI * W, W)
        slab_batch = jnp.take(slab_matrix, jnp.take(block_irrep, chosen), axis=1)
        return jnp.einsum("pbk,bkw->bpw", slab_batch.astype(jnp.float32), tile_batch.astype(jnp.float32))

    products = lax.map(one_batch, block_ids.reshape(NB // batch_size, batch_size)).reshape(NB, PAIRS, W)
    facing = jnp.take(products, partner, axis=0)
    mirrored = jnp.roll(facing, PAIRS // 2, axis=1)
    summed = products + sign.astype(jnp.float32)[:, None, None] * mirrored
    return jnp.transpose(summed.astype(jnp.bfloat16), (1, 0, 2)).reshape(PAIRS, NB * W)
```

```python
import jax
import jax.numpy as jnp
from jax import lax
from jax.experimental import pallas as pl
from jax.experimental.pallas import tpu as pltpu
from jax.sharding import PartitionSpec as P

BOTH = ("blk", "pair")
TOP = 32760.0
STEPS = 64.0
LN2 = 0.6931471805599453
MIB = 1 << 20


def call(body, grid, prefetch, ins, outs, shapes, scratch, vmem, cost):
    spec = pltpu.PrefetchScalarGridSpec(
        num_scalar_prefetch=prefetch, grid=grid, in_specs=ins, out_specs=outs, scratch_shapes=scratch
    )
    return pl.pallas_call(
        body,
        grid_spec=spec,
        out_shape=shapes,
        compiler_params=pltpu.CompilerParams(vmem_limit_bytes=vmem),
        cost_estimate=pl.CostEstimate(flops=cost[0], bytes_accessed=cost[1], transcendentals=0),
    )


def whole(shape):
    return pl.BlockSpec(shape, lambda i, *_: (0,) * len(shape))


def extract_body(where_ref, amp_ref, out_ref):
    for n in range(32):
        place = where_ref[n]
        start = pl.multiple_of(jnp.maximum(place, 0) * 128, 128)
        tile = amp_ref[:, pl.ds(start, 128)]
        held = jnp.where(place >= 0, tile, jnp.zeros_like(tile))
        out_ref[n // 2, :, (n % 2) * 128 : (n % 2) * 128 + 128] = held


def merge_body(in_ref, out_ref):
    total = in_ref[0].astype(jnp.float32)
    for s in range(1, 16):
        total += in_ref[s].astype(jnp.float32)
    part = total.astype(jnp.bfloat16)
    for s in range(64):
        out_ref[s] = part


def row_tiles(p):
    return (2 * p, 2 * p + 8) if p < 4 else (2 * (p - 4) + 9, 2 * (p - 4) + 1)


def product_body(irrep_ref, core_ref, mine_ref, other_ref, tile_ref, out_ref, slab, prod, peak, code):
    step = pl.program_id(0)

    @pl.when(step == 0)
    def _():
        core = core_ref[0]
        for source, shift in ((mine_ref, core), (other_ref, 1 - core)):
            for c in range(16):
                for x in range(4):
                    rows = pl.ds(pl.multiple_of((2 * x + shift) * 16, 16), 16)
                    slab[c // 2, rows, (c % 2) * 256 : (c % 2) * 256 + 256] = source[c * 4 + x]
        peak[...] = jnp.zeros_like(peak)

    @pl.when(step < 16)
    def _():
        top = peak[...]
        for k in range(5):
            slot = step * 5 + k
            irrep = irrep_ref[slot]
            left = slab[jnp.maximum(irrep, 0)]
            right = tile_ref[k].reshape(512, 128)
            value = jnp.dot(left, right, preferred_element_type=jnp.float32)
            prod[slot] = value
            high = jnp.max(jnp.abs(value).reshape(16, 8, 128), axis=0)
            top = jnp.maximum(top, jnp.where(irrep >= 0, high, 0.0))
        peak[...] = top

    @pl.when(step == 16)
    def _():
        top = jnp.max(jnp.max(peak[...], axis=1, keepdims=True), axis=0, keepdims=True)
        level = jnp.ceil(jnp.log(jnp.maximum(top, 1e-30)) * (STEPS / LN2))
        code[...] = jnp.broadcast_to(level, (8, 128)).astype(jnp.int32)

    @pl.when(step >= 16)
    def _():
        level = code[...]
        inverse = jnp.exp(level.astype(jnp.float32) * (-LN2 / STEPS)) * TOP
        for k in range(5):
            slot = (step - 16) * 5 + k
            for p in range(8):
                words = []
                for u in row_tiles(p):
                    value = prod[slot, u * 8 : u * 8 + 8, :]
                    words.append(jnp.floor(value * inverse + 0.5).astype(jnp.int32))
                out_ref[0, p, k] = (words[0] << 16) | (words[1] & 0xFFFF)
        for p in range(8):
            out_ref[0, p, 5] = level


def select_body(from_ref, to_ref, in_ref, out_ref):
    def one(j, carry):
        out_ref[to_ref[j]] = in_ref[from_ref[j]]
        return carry

    lax.fori_loop(0, 256, one, 0, unroll=8)


def combine_body(own_ref, own_scale_ref, face_ref, face_scale_ref, sign_ref, here_ref, there_ref, keep_ref, send_ref):
    def scale(index):
        return jnp.exp(here_ref[index].astype(jnp.float32) * (LN2 / STEPS)) * (1.0 / TOP)

    def one(j, carry):
        own = here_ref[own_ref[j]]
        face = there_ref[face_ref[j]]
        own_scale = scale(own_scale_ref[j])
        face_scale = scale(face_scale_ref[j]) * sign_ref[j].astype(jnp.float32)
        own_high = (own >> 16).astype(jnp.float32)
        own_low = ((own << 16) >> 16).astype(jnp.float32)
        face_high = (face >> 16).astype(jnp.float32)
        face_low = ((face << 16) >> 16).astype(jnp.float32)
        columns = pl.ds(pl.multiple_of(j * 128, 128), 128)
        keep_ref[:, columns] = (own_high * own_scale + face_low * face_scale).astype(jnp.bfloat16)
        send_ref[:, columns] = (own_low * own_scale + face_high * face_scale).astype(jnp.bfloat16)
        return carry

    lax.fori_loop(0, 256, one, 0, unroll=4)


def local(amplitudes, integrals, block_irrep, slab_blocks, owner, partner, sign):
    blk = lax.axis_index("blk")
    pair = lax.axis_index("pair")
    me = blk * 8 + pair
    int32 = jnp.int32

    where = jnp.where(slab_blocks // 256 == blk, slab_blocks % 256, -1).astype(int32)
    parts = call(
        extract_body, (1,), 1, [whole((16, 32768))], whole((16, 16, 256)),
        jax.ShapeDtypeStruct((16, 16, 256), jnp.bfloat16), [], 8 * MIB, (0, 1 << 20),
    )(where, amplitudes)
    parts = lax.all_to_all(parts, "blk", split_axis=0, concat_axis=0, tiled=True)
    copies = call(
        merge_body, (1,), 0, [whole((16, 16, 256))], whole((64, 16, 256)),
        jax.ShapeDtypeStruct((64, 16, 256), jnp.bfloat16), [], 8 * MIB, (0, 1 << 20),
    )(parts)
    groups = [[c + 2 * i for i in range(64)] for c in range(2)]
    mine = lax.all_to_all(copies, BOTH, split_axis=0, concat_axis=0, tiled=True, axis_index_groups=groups)
    other = lax.ppermute(mine, "pair", [(i, i ^ 1) for i in range(8)])

    ids = jnp.arange(256, dtype=int32)
    stored = (owner == me).reshape(16, 256)
    earlier = (ids[:, None] < ids[None, :]).astype(jnp.bfloat16)
    slot_rank = jnp.dot(stored.astype(jnp.bfloat16), earlier, preferred_element_type=jnp.float32).astype(int32)
    labels = block_irrep.reshape(16, 256) + 1
    chosen = stored[:, None, :] & (slot_rank[:, None, :] == jnp.arange(5, dtype=int32)[None, :, None])
    slot_irrep = (jnp.sum(jnp.where(chosen, labels[:, None, :], 0), axis=2) - 1).reshape(80)

    my_owner = lax.dynamic_slice_in_dim(owner, blk * 256, 256)
    my_partner = lax.dynamic_slice_in_dim(partner, blk * 256, 256)
    my_sign = lax.dynamic_slice_in_dim(sign, blk * 256, 256)
    before = ids[None, :] < ids[:, None]
    rank = jnp.sum((my_owner[None, :] == my_owner[:, None]) & before, axis=1).astype(int32)
    arrive = my_owner * 6 + rank
    target = my_partner // 256
    leave_key = target * 256 + ids
    leave = jnp.sum(leave_key[None, :] < leave_key[:, None], axis=1).astype(int32)
    back = jnp.sum(my_partner[None, :] < my_partner[:, None], axis=1).astype(int32)
    all_ids = jnp.arange(4096, dtype=int32)
    face_owner = jnp.sum(jnp.where(my_partner[:, None] == all_ids[None, :], owner[None, :], 0), axis=1)

    core = (pair % 2).reshape(1).astype(int32)
    coded = call(
        product_body, (32,), 2,
        [
            whole((64, 16, 256)),
            whole((64, 16, 256)),
            pl.BlockSpec((5, 4, 128, 128), lambda i, *_: (jnp.minimum(i, 15), 0, 0, 0)),
        ],
        pl.BlockSpec((1, 8, 6, 8, 128), lambda i, *_: (jnp.maximum(i - 16, 0), 0, 0, 0, 0)),
        jax.ShapeDtypeStruct((16, 8, 6, 8, 128), int32),
        [
            pltpu.VMEM((8, 128, 512), jnp.bfloat16),
            pltpu.VMEM((80, 128, 128), jnp.float32),
            pltpu.VMEM((8, 128), jnp.float32),
            pltpu.VMEM((8, 128), int32),
        ],
        24 * MIB, (1_342_177_280, 14 << 20),
    )(slot_irrep, core, mine, other, integrals)
    arrived = lax.all_to_all(coded.reshape(128, 48, 128), BOTH, split_axis=0, concat_axis=0, tiled=True)
    arrived = arrived.reshape(768, 8, 128)
    outgoing = call(
        select_body, (1,), 2, [whole((768, 8, 128))], whole((256, 8, 128)),
        jax.ShapeDtypeStruct((256, 8, 128), int32), [], 16 * MIB, (0, 4 << 20),
    )(arrive, leave, arrived)
    incoming = lax.all_to_all(outgoing, "blk", split_axis=0, concat_axis=0, tiled=True)
    half = jax.ShapeDtypeStruct((8, 32768), jnp.bfloat16)
    keep, send = call(
        combine_body, (1,), 5, [whole((768, 8, 128)), whole((256, 8, 128))],
        [whole((8, 32768)), whole((8, 32768))], [half, half], [], 16 * MIB, (0, 5 << 20),
    )(arrive, my_owner * 6 + 5, back, face_owner * 6 + 5, my_sign, arrived, incoming)
    got = lax.ppermute(send, "pair", [(i, i ^ 4) for i in range(8)])
    first = pair < 4
    return jnp.concatenate([jnp.where(first, keep, got), jnp.where(first, got, keep)], axis=0)


def solution(mesh):
    placed = (P("pair", "blk"), P(BOTH, None, None, None), P(), P(), P(), P(), P())
    return jax.shard_map(local, mesh=mesh, in_specs=placed, out_specs=P("pair", "blk"), check_vma=False)
```

```python
import jax
import jax.numpy as jnp
from jax import lax
from jax.experimental import pallas as pl
from jax.experimental.pallas import tpu as pltpu
from jax.sharding import PartitionSpec as P

BOTH = ("blk", "pair")
TOP = 32760.0
STEPS = 64.0
LN2 = 0.6931471805599453
MIB = 1 << 20
VMEM = pl.BlockSpec(memory_space=pltpu.VMEM)
HBM = pl.BlockSpec(memory_space=pltpu.HBM)
SMEM = pl.BlockSpec(memory_space=pltpu.SMEM)


def call(body, ins, outs, shapes, scratch, vmem, flops, moved):
    return pl.pallas_call(
        body,
        in_specs=ins,
        out_specs=outs,
        out_shape=shapes,
        scratch_shapes=scratch,
        compiler_params=pltpu.CompilerParams(vmem_limit_bytes=vmem),
        cost_estimate=pl.CostEstimate(flops=flops, bytes_accessed=moved, transcendentals=0),
    )


def extract_body(blocks_ref, amp_ref, out_ref, sems):
    blk = lax.axis_index("blk")

    def move(n):
        start = pl.multiple_of((blocks_ref[n] & 255) * 128, 128)
        return pltpu.make_async_copy(
            amp_ref.at[:, pl.ds(start, 128)],
            out_ref.at[n // 2, :, pl.ds((n % 2) * 128, 128)],
            sems.at[n],
        )

    for n in range(32):
        held = (blocks_ref[n] >> 8) == blk

        @pl.when(held)
        def _():
            move(n).start()

        @pl.when(jnp.logical_not(held))
        def _():
            out_ref[n // 2, :, (n % 2) * 128 : (n % 2) * 128 + 128] = jnp.zeros((16, 128), jnp.bfloat16)

    for n in range(32):

        @pl.when((blocks_ref[n] >> 8) == blk)
        def _():
            move(n).wait()


def merge_body(in_ref, out_ref):
    total = in_ref[0].astype(jnp.float32)
    for s in range(1, 16):
        total += in_ref[s].astype(jnp.float32)
    part = total.astype(jnp.bfloat16)
    for s in range(64):
        out_ref[s] = part


def row_tiles(p):
    return (2 * p, 2 * p + 8) if p < 4 else (2 * (p - 4) + 9, 2 * (p - 4) + 1)


def product_body(irrep_ref, mine_ref, other_ref, tiles_ref, out_ref, level_ref, held, slab, prod, code, in_sems, out_sems):
    def fetch(t):
        span = pl.ds(t * 5, 5)
        return pltpu.make_async_copy(tiles_ref.at[span], held.at[span], in_sems.at[t])

    def store(t):
        return pltpu.make_async_copy(code.at[t], out_ref.at[t], out_sems.at[t])

    for t in range(16):
        fetch(t).start()
    core = lax.axis_index("pair") % 2
    for source, shift in ((mine_ref, core), (other_ref, 1 - core)):
        for c in range(16):
            for x in range(4):
                rows = pl.ds(pl.multiple_of((2 * x + shift) * 16, 16), 16)
                slab[c // 2, rows, (c % 2) * 256 : (c % 2) * 256 + 256] = source[c * 4 + x]

    def multiply(t, top):
        fetch(t).wait()
        for k in range(5):
            slot = t * 5 + k
            irrep = irrep_ref[slot]
            left = slab[jnp.maximum(irrep, 0)]
            right = held[slot].reshape(512, 128)
            value = jnp.dot(left, right, preferred_element_type=jnp.float32)
            prod[slot] = value
            high = jnp.max(jnp.abs(value).reshape(16, 8, 128), axis=0)
            top = jnp.maximum(top, jnp.where(irrep >= 0, high, 0.0))
        return top

    top = lax.fori_loop(0, 16, multiply, jnp.zeros((8, 128), jnp.float32))
    top = jnp.max(jnp.max(top, axis=1, keepdims=True), axis=0, keepdims=True)
    level = jnp.ceil(jnp.log(jnp.maximum(top, 1e-30)) * (STEPS / LN2))
    level = jnp.broadcast_to(level, (8, 128))
    level_ref[...] = level.astype(jnp.int32)
    inverse = jnp.exp(level * (-LN2 / STEPS)) * TOP

    def quantise(t, carry):
        for k in range(5):
            for p in range(8):
                high, low = (
                    jnp.floor(prod[t * 5 + k, u * 8 : u * 8 + 8, :] * inverse + 0.5).astype(jnp.int32) for u in row_tiles(p)
                )
                code[t, p, k] = (high << 16) | (low & 0xFFFF)
        store(t).start()
        return carry

    lax.fori_loop(0, 16, quantise, 0)
    for t in range(16):
        store(t).wait()


def select_body(from_ref, in_ref, level_ref, out_ref):
    def one(t, carry):
        for i in range(16):
            out_ref[t, i] = in_ref[from_ref[t * 16 + i]]
        out_ref[t, 16] = level_ref[...]
        return carry

    lax.fori_loop(0, 16, one, 0)


def combine(index_ref, here_ref, there_ref, table, out_ref, own_part, face_part):
    def one(step, carry):
        for i in range(8):
            j = step * 8 + i
            own = own_part(here_ref[index_ref[0, j]]).astype(jnp.float32)
            face = face_part(there_ref[index_ref[1, j]]).astype(jnp.float32)
            face_scale = table[index_ref[3, j]] * index_ref[4, j].astype(jnp.float32)
            value = own * table[index_ref[2, j]] + face * face_scale
            out_ref[:, pl.ds(pl.multiple_of(j * 128, 128), 128)] = value.astype(jnp.bfloat16)
        return carry

    lax.fori_loop(0, 32, one, 0)


def high_part(word):
    return word >> 16


def low_part(word):
    return (word << 16) >> 16


def send_body(index_ref, here_ref, there_ref, out_ref, table_ref):
    for s in range(16):
        scale = jnp.exp(there_ref[s * 17 + 16].astype(jnp.float32) * (LN2 / STEPS)) * (1.0 / TOP)
        for r in range(8):
            table_ref[s * 8 + r] = jnp.broadcast_to(scale[r : r + 1, :], (8, 128))
    combine(index_ref, here_ref, there_ref, table_ref, out_ref, low_part, high_part)


def keep_body(index_ref, here_ref, there_ref, table_ref, out_ref):
    combine(index_ref, here_ref, there_ref, table_ref, out_ref, high_part, low_part)


def swap(value, mask):
    return lax.ppermute(value, "pair", [(i, i ^ mask) for i in range(8)])


def local(amplitudes, integrals, block_irrep, slab_blocks, owner, partner, sign):
    blk = lax.axis_index("blk")
    pair = lax.axis_index("pair")
    me = blk * 8 + pair
    int32 = jnp.int32
    dma = pltpu.SemaphoreType.DMA

    parts = call(
        extract_body, [SMEM, HBM], VMEM, jax.ShapeDtypeStruct((16, 16, 256), jnp.bfloat16), [dma((32,))], 60 * MIB, 0, 1 << 18
    )(slab_blocks, amplitudes)
    parts = lax.all_to_all(parts, "blk", split_axis=0, concat_axis=0, tiled=True)
    copies = call(
        merge_body, [VMEM], VMEM, jax.ShapeDtypeStruct((64, 16, 256), jnp.bfloat16), [], 4 * MIB, 0, 1 << 20
    )(parts)
    groups = [[c + 2 * i for i in range(64)] for c in range(2)]
    mine = lax.all_to_all(copies, BOTH, split_axis=0, concat_axis=0, tiled=True, axis_index_groups=groups)
    other = swap(mine, 1)

    ids = jnp.arange(256, dtype=int32)
    stored = (owner == me).reshape(16, 256)
    earlier = (ids[:, None] < ids[None, :]).astype(jnp.bfloat16)
    slot_rank = jnp.dot(stored.astype(jnp.bfloat16), earlier, preferred_element_type=jnp.float32).astype(int32)
    labels = block_irrep.reshape(16, 256) + 1
    chosen = stored[:, None, :] & (slot_rank[:, None, :] == jnp.arange(5, dtype=int32)[None, :, None])
    slot_irrep = (jnp.sum(jnp.where(chosen, labels[:, None, :], 0), axis=2) - 1).reshape(80)

    my_owner = lax.dynamic_slice_in_dim(owner, blk * 256, 256)
    my_partner = lax.dynamic_slice_in_dim(partner, blk * 256, 256)
    my_sign = lax.dynamic_slice_in_dim(sign, blk * 256, 256)
    before = ids[None, :] < ids[:, None]
    rank = jnp.sum((my_owner[None, :] == my_owner[:, None]) & before, axis=1).astype(int32)
    arrive = my_owner * 5 + rank
    leave_key = (my_partner // 256) * 256 + ids
    leave = jnp.sum(leave_key[None, :] < leave_key[:, None], axis=1).astype(int32)
    leaving = jnp.sum(jnp.where(leave[None, :] == ids[:, None], arrive[None, :], 0), axis=1).astype(int32)
    back = jnp.sum(my_partner[None, :] < my_partner[:, None], axis=1).astype(int32)
    all_ids = jnp.arange(4096, dtype=int32)
    face_owner = jnp.sum(jnp.where(my_partner[:, None] == all_ids[None, :], owner[None, :], 0), axis=1)
    index = jnp.stack([arrive, back + back // 16, my_owner ^ pair, face_owner ^ pair, my_sign])

    coded, level = call(
        product_body, [SMEM, VMEM, VMEM, HBM], [HBM, VMEM],
        [jax.ShapeDtypeStruct((16, 8, 5, 8, 128), int32), jax.ShapeDtypeStruct((8, 128), int32)],
        [
            pltpu.VMEM((80, 4, 128, 128), jnp.bfloat16),
            pltpu.VMEM((8, 128, 512), jnp.bfloat16),
            pltpu.VMEM((80, 128, 128), jnp.float32),
            pltpu.VMEM((16, 8, 5, 8, 128), int32),
            dma((16,)),
            dma((16,)),
        ],
        52 * MIB, 1_342_177_280, 14 << 20,
    )(slot_irrep, mine, other, integrals)
    arrived = lax.all_to_all(coded.reshape(128, 40, 128), BOTH, split_axis=0, concat_axis=0, tiled=True)
    arrived = arrived.reshape(640, 8, 128)
    levels = level[:1]
    for mask in (1, 2, 4):
        levels = jnp.concatenate([levels, swap(levels, mask)], axis=0)
    outgoing = call(
        select_body, [SMEM, VMEM, VMEM], VMEM, jax.ShapeDtypeStruct((16, 17, 8, 128), int32), [], 16 * MIB, 0, 3 << 20
    )(leaving, arrived, levels)
    incoming = lax.all_to_all(outgoing, "blk", split_axis=0, concat_axis=0, tiled=True).reshape(272, 8, 128)
    half = jax.ShapeDtypeStruct((8, 32768), jnp.bfloat16)
    send, table = call(
        send_body, [SMEM, VMEM, VMEM], [VMEM, VMEM], [half, jax.ShapeDtypeStruct((128, 8, 128), jnp.float32)],
        [], 16 * MIB, 0, 4 << 20,
    )(index, arrived, incoming)
    got = swap(send, 4)
    keep = call(
        keep_body, [SMEM, VMEM, VMEM, VMEM], VMEM, half, [], 16 * MIB, 0, 4 << 20
    )(index, arrived, incoming, table)
    kept = (lax.broadcasted_iota(int32, (2, 1, 1), 0) == pair // 4)
    return jnp.where(kept, keep[None], got[None]).reshape(16, 32768)


def solution(mesh):
    placed = (P("pair", "blk"), P(BOTH, None, None, None), P(), P(), P(), P(), P())
    return jax.shard_map(local, mesh=mesh, in_specs=placed, out_specs=P("pair", "blk"), check_vma=False)
```

```python
import jax
import jax.numpy as jnp
from jax import lax
from jax.experimental import pallas as pl
from jax.experimental.pallas import tpu as pltpu
from jax.sharding import PartitionSpec as P

BOTH = ("blk", "pair")
TOP = 32760.0
STEPS = 64.0
LN2 = 0.6931471805599453
MIB = 1 << 20
GROUP = 4
VMEM = pl.BlockSpec(memory_space=pltpu.VMEM)
HBM = pl.BlockSpec(memory_space=pltpu.HBM)
SMEM = pl.BlockSpec(memory_space=pltpu.SMEM)


def call(body, ins, outs, shapes, scratch, vmem, flops, moved):
    return pl.pallas_call(
        body,
        in_specs=ins,
        out_specs=outs,
        out_shape=shapes,
        scratch_shapes=scratch,
        compiler_params=pltpu.CompilerParams(vmem_limit_bytes=vmem),
        cost_estimate=pl.CostEstimate(flops=flops, bytes_accessed=moved, transcendentals=0),
    )


def extract_body(blocks_ref, amp_ref, out_ref, sems):
    blk = lax.axis_index("blk")

    def move(n):
        start = pl.multiple_of((blocks_ref[n] & 255) * 128, 128)
        return pltpu.make_async_copy(
            amp_ref.at[:, pl.ds(start, 128)],
            out_ref.at[n // 2, :, pl.ds((n % 2) * 128, 128)],
            sems.at[n],
        )

    for n in range(32):
        held = (blocks_ref[n] >> 8) == blk

        @pl.when(held)
        def _():
            move(n).start()

        @pl.when(jnp.logical_not(held))
        def _():
            out_ref[n // 2, :, (n % 2) * 128 : (n % 2) * 128 + 128] = jnp.zeros((16, 128), jnp.bfloat16)

    for n in range(32):

        @pl.when((blocks_ref[n] >> 8) == blk)
        def _():
            move(n).wait()


def merge_body(in_ref, out_ref):
    total = in_ref[0].astype(jnp.float32)
    for s in range(1, 16):
        total += in_ref[s].astype(jnp.float32)
    part = total.astype(jnp.bfloat16)
    for s in range(64):
        out_ref[s] = part


def row_tiles(p):
    return (2 * p, 2 * p + 8) if p < 4 else (2 * (p - 4) + 9, 2 * (p - 4) + 1)


def product_body(irrep_ref, mine_ref, other_ref, tiles_ref, out_ref, level_ref, held, slab, prod, code, in_sems, out_sems):
    def fetch(t):
        span = pl.ds(t * 5, 5)
        return pltpu.make_async_copy(tiles_ref.at[span], held.at[span], in_sems.at[t])

    def store(t):
        return pltpu.make_async_copy(code.at[t], out_ref.at[t], out_sems.at[t])

    for t in range(16):
        fetch(t).start()
    core = lax.axis_index("pair") % 2
    for source, shift in ((mine_ref, core), (other_ref, 1 - core)):
        for c in range(16):
            for x in range(4):
                rows = pl.ds(pl.multiple_of((2 * x + shift) * 16, 16), 16)
                slab[c // 2, rows, (c % 2) * 256 : (c % 2) * 256 + 256] = source[c * 4 + x]

    def multiply(step, top):
        for t in range(GROUP):
            fetch(step * GROUP + t).wait()
        count = GROUP * 5
        values = []
        for k in range(count + 1):
            if k < count:
                slot = step * count + k
                left = slab[jnp.maximum(irrep_ref[slot], 0)]
                right = held[slot].reshape(512, 128)
                values.append(jnp.dot(left, right, preferred_element_type=jnp.float32))
            if k > 0:
                slot = step * count + k - 1
                value = values[k - 1]
                prod[slot] = value
                high = jnp.max(jnp.abs(value).reshape(16, 8, 128), axis=0)
                top = jnp.maximum(top, jnp.where(irrep_ref[slot] >= 0, high, 0.0))
        return top

    top = lax.fori_loop(0, 16 // GROUP, multiply, jnp.zeros((8, 128), jnp.float32))
    top = jnp.max(jnp.max(top, axis=1, keepdims=True), axis=0, keepdims=True)
    level = jnp.ceil(jnp.log(jnp.maximum(top, 1e-30)) * (STEPS / LN2))
    level = jnp.broadcast_to(level, (8, 128))
    level_ref[...] = level.astype(jnp.int32)
    inverse = jnp.exp(level * (-LN2 / STEPS)) * TOP

    def quantise(t, carry):
        for k in range(5):
            value = prod[t * 5 + k]
            words = []
            for p in range(8):
                high, low = (
                    jnp.floor(value[u * 8 : u * 8 + 8, :] * inverse + 0.5).astype(jnp.int32) for u in row_tiles(p)
                )
                words.append((high << 16) | (low & 0xFFFF))
            for p in range(8):
                code[t, p, k] = words[p]
        store(t).start()
        return carry

    lax.fori_loop(0, 16, quantise, 0)
    for t in range(16):
        store(t).wait()


def select_body(from_ref, in_ref, level_ref, out_ref, picked, sems):
    def store(c):
        span = pl.ds(c * 4, 4)
        return pltpu.make_async_copy(picked.at[span], out_ref.at[span], sems.at[c])

    def one(t, carry):
        for i in range(16):
            picked[t, i] = in_ref[from_ref[t * 16 + i]]
        picked[t, 16] = level_ref[...]
        return carry

    for c in range(4):
        lax.fori_loop(c * 4, c * 4 + 4, one, 0)
        store(c).start()
    for c in range(4):
        store(c).wait()


def gather_body(from_ref, in_ref, out_ref, picked, sems):
    def one(step, carry):
        for i in range(16):
            picked[step * 16 + i] = in_ref[from_ref[step * 16 + i]]
        return carry

    lax.fori_loop(0, 16, one, 0)
    store = pltpu.make_async_copy(picked, out_ref, sems.at[0])
    store.start()
    store.wait()


def combine(back_ref, own_ref, there_ref, scale_ref, out_ref, own_part, face_part):
    def one(step, carry):
        rows = pl.multiple_of(step * 8, 8)
        own_scale = scale_ref[pl.ds(rows, 8), :]
        face_scale = scale_ref[pl.ds(256 + rows, 8), :]
        values = []
        for i in range(8):
            own = own_part(own_ref[step * 8 + i]).astype(jnp.float32)
            face = face_part(there_ref[back_ref[step * 8 + i]]).astype(jnp.float32)
            values.append((own * own_scale[i : i + 1, :] + face * face_scale[i : i + 1, :]).astype(jnp.bfloat16))
        for i in range(8):
            out_ref[:, pl.ds(pl.multiple_of((step * 8 + i) * 128, 128), 128)] = values[i]
        return carry

    lax.fori_loop(0, 32, one, 0)


def high_part(word):
    return word >> 16


def low_part(word):
    return (word << 16) >> 16


def send_body(back_ref, own_ref, there_ref, pick_ref, sign_ref, out_ref, scale_ref):
    levels = jnp.concatenate([there_ref[s * 17 + 16] for s in range(16)], axis=0)
    pick = pick_ref[...]
    upper = jnp.dot(pick, (levels >> 5).astype(jnp.bfloat16), preferred_element_type=jnp.float32)
    lower = jnp.dot(pick, (levels & 31).astype(jnp.bfloat16), preferred_element_type=jnp.float32)
    scale_ref[...] = jnp.exp((upper * 32.0 + lower) * (LN2 / STEPS)) * (1.0 / TOP) * sign_ref[...]
    combine(back_ref, own_ref, there_ref, scale_ref, out_ref, low_part, high_part)


def keep_body(back_ref, own_ref, there_ref, scale_ref, out_ref):
    combine(back_ref, own_ref, there_ref, scale_ref, out_ref, high_part, low_part)


def finish_body(keep_ref, got_ref, out_ref):
    first = lax.axis_index("pair") < 4
    keep = keep_ref[...]
    got = got_ref[...]
    out_ref[0:8, :] = jnp.where(first, keep, got)
    out_ref[8:16, :] = jnp.where(first, got, keep)


def call_product(irreps, mine, other, tiles):
    dma = pltpu.SemaphoreType.DMA
    int32 = jnp.int32
    return call(
        product_body, [SMEM, VMEM, VMEM, HBM], [HBM, VMEM],
        [pltpu.HBM((16, 8, 5, 8, 128), int32), jax.ShapeDtypeStruct((8, 128), int32)],
        [
            pltpu.VMEM((80, 4, 128, 128), jnp.bfloat16),
            pltpu.VMEM((8, 128, 512), jnp.bfloat16),
            pltpu.VMEM((80, 128, 128), jnp.float32),
            pltpu.VMEM((16, 8, 5, 8, 128), int32),
            dma((16,)),
            dma((16,)),
        ],
        52 * MIB, 1_342_177_280, 14 << 20,
    )(irreps, mine, other, tiles)


HALF = jax.ShapeDtypeStruct((8, 32768), jnp.bfloat16)


def call_send(back, own, there, pick, signs):
    scale = jax.ShapeDtypeStruct((512, 128), jnp.float32)
    return call(send_body, [SMEM] + [VMEM] * 4, [VMEM, VMEM], [HALF, scale], [], 16 * MIB, 0, 4 << 20)(
        back, own, there, pick, signs
    )


def call_keep(back, own, there, scale):
    return call(keep_body, [SMEM] + [VMEM] * 3, VMEM, HALF, [], 16 * MIB, 0, 4 << 20)(back, own, there, scale)


def call_finish(keep, got):
    half = pl.BlockSpec((8, 16384), lambda i: (0, i))
    return pl.pallas_call(
        finish_body,
        grid=(2,),
        in_specs=[half, half],
        out_specs=pl.BlockSpec((16, 16384), lambda i: (0, i)),
        out_shape=jax.ShapeDtypeStruct((16, 32768), jnp.bfloat16),
        compiler_params=pltpu.CompilerParams(vmem_limit_bytes=16 * MIB),
        cost_estimate=pl.CostEstimate(flops=0, bytes_accessed=2 << 20, transcendentals=0),
    )(keep, got)


def swap(value, mask):
    return lax.ppermute(value, "pair", [(i, i ^ mask) for i in range(8)])


def local(amplitudes, integrals, block_irrep, slab_blocks, owner, partner, sign):
    blk = lax.axis_index("blk")
    pair = lax.axis_index("pair")
    me = blk * 8 + pair
    int32 = jnp.int32
    dma = pltpu.SemaphoreType.DMA

    parts = call(
        extract_body, [SMEM, HBM], VMEM, jax.ShapeDtypeStruct((16, 16, 256), jnp.bfloat16), [dma((32,))], 60 * MIB, 0, 1 << 18
    )(slab_blocks, amplitudes)
    parts = lax.all_to_all(parts, "blk", split_axis=0, concat_axis=0, tiled=True)
    copies = call(
        merge_body, [VMEM], VMEM, jax.ShapeDtypeStruct((64, 16, 256), jnp.bfloat16), [], 4 * MIB, 0, 1 << 20
    )(parts)
    groups = [[c + 2 * i for i in range(64)] for c in range(2)]
    mine = lax.all_to_all(copies, BOTH, split_axis=0, concat_axis=0, tiled=True, axis_index_groups=groups)
    other = swap(mine, 1)

    ids = jnp.arange(256, dtype=int32)
    stored = (owner == me).reshape(16, 256)
    earlier = (ids[:, None] < ids[None, :]).astype(jnp.bfloat16)
    slot_rank = jnp.dot(stored.astype(jnp.bfloat16), earlier, preferred_element_type=jnp.float32).astype(int32)
    labels = block_irrep.reshape(16, 256) + 1
    chosen = stored[:, None, :] & (slot_rank[:, None, :] == jnp.arange(5, dtype=int32)[None, :, None])
    slot_irrep = (jnp.sum(jnp.where(chosen, labels[:, None, :], 0), axis=2) - 1).reshape(80)

    my_owner = lax.dynamic_slice_in_dim(owner, blk * 256, 256)
    my_partner = lax.dynamic_slice_in_dim(partner, blk * 256, 256)
    my_sign = lax.dynamic_slice_in_dim(sign, blk * 256, 256)
    before = ids[None, :] < ids[:, None]
    rank = jnp.sum((my_owner[None, :] == my_owner[:, None]) & before, axis=1).astype(int32)
    arrive = my_owner * 5 + rank
    leave_key = (my_partner // 256) * 256 + ids
    leave = jnp.sum(leave_key[None, :] < leave_key[:, None], axis=1).astype(int32)
    leaving = jnp.sum(jnp.where(leave[None, :] == ids[:, None], arrive[None, :], 0), axis=1).astype(int32)
    back = jnp.sum(my_partner[None, :] < my_partner[:, None], axis=1).astype(int32)
    all_ids = jnp.arange(4096, dtype=int32)
    face_owner = jnp.sum(jnp.where(my_partner[:, None] == all_ids[None, :], owner[None, :], 0), axis=1)
    back = back + back // 16
    rows = jnp.concatenate([my_owner ^ pair, face_owner ^ pair])
    pick = (rows[:, None] == jnp.arange(128, dtype=int32)[None, :]).astype(jnp.bfloat16)
    signs = jnp.concatenate([jnp.ones_like(my_sign), my_sign]).astype(jnp.float32)
    signs = jnp.broadcast_to(signs[:, None], (512, 128))

    coded, level = call_product(slot_irrep, mine, other, integrals)
    arrived = lax.all_to_all(coded.reshape(128, 40, 128), BOTH, split_axis=0, concat_axis=0, tiled=True)
    arrived = arrived.reshape(640, 8, 128)
    levels = level[:1]
    for mask in (1, 2, 4):
        levels = jnp.concatenate([levels, swap(levels, mask)], axis=0)
    outgoing = call(
        select_body, [SMEM, VMEM, VMEM], HBM, pltpu.HBM((16, 17, 8, 128), int32),
        [pltpu.VMEM((16, 17, 8, 128), int32), dma((4,))], 16 * MIB, 0, 3 << 20,
    )(leaving, arrived, levels)
    incoming = lax.all_to_all(outgoing, "blk", split_axis=0, concat_axis=0, tiled=True).reshape(272, 8, 128)
    own = call(
        gather_body, [SMEM, VMEM], HBM, pltpu.HBM((256, 8, 128), int32), [pltpu.VMEM((256, 8, 128), int32), dma((1,))], 16 * MIB, 0, 2 << 20
    )(arrive, arrived)
    send, scale = call_send(back, own, incoming, pick, signs)
    got = swap(send, 4)
    keep = call_keep(back, own, incoming, scale)
    return call_finish(keep, got)


def solution(mesh):
    placed = (P("pair", "blk"), P(BOTH, None, None, None), P(), P(), P(), P(), P())
    return jax.shard_map(local, mesh=mesh, in_specs=placed, out_specs=P("pair", "blk"), check_vma=False)
```

```python
import jax
import jax.numpy as jnp
from jax import lax
from jax.experimental import pallas as pl
from jax.experimental.pallas import tpu as pltpu
from jax.sharding import PartitionSpec as P

BOTH = ("blk", "pair")
TOP = 32760.0
STEPS = 64.0
LN2 = 0.6931471805599453
MIB = 1 << 20
GROUP = 4
VMEM = pl.BlockSpec(memory_space=pltpu.VMEM)
HBM = pl.BlockSpec(memory_space=pltpu.HBM)
SMEM = pl.BlockSpec(memory_space=pltpu.SMEM)


def call(body, ins, outs, shapes, scratch, vmem, flops, moved):
    return pl.pallas_call(
        body,
        in_specs=ins,
        out_specs=outs,
        out_shape=shapes,
        scratch_shapes=scratch,
        compiler_params=pltpu.CompilerParams(vmem_limit_bytes=vmem),
        cost_estimate=pl.CostEstimate(flops=flops, bytes_accessed=moved, transcendentals=0),
    )


def extract_body(blocks_ref, amp_ref, out_ref, sems):
    blk = lax.axis_index("blk")

    def move(n):
        start = pl.multiple_of((blocks_ref[n] & 255) * 128, 128)
        return pltpu.make_async_copy(
            amp_ref.at[:, pl.ds(start, 128)],
            out_ref.at[n // 2, :, pl.ds((n % 2) * 128, 128)],
            sems.at[n],
        )

    for n in range(32):
        held = (blocks_ref[n] >> 8) == blk

        @pl.when(held)
        def _():
            move(n).start()

        @pl.when(jnp.logical_not(held))
        def _():
            out_ref[n // 2, :, (n % 2) * 128 : (n % 2) * 128 + 128] = jnp.zeros((16, 128), jnp.bfloat16)

    for n in range(32):

        @pl.when((blocks_ref[n] >> 8) == blk)
        def _():
            move(n).wait()


def merge_body(in_ref, out_ref):
    total = in_ref[0].astype(jnp.float32)
    for s in range(1, 16):
        total += in_ref[s].astype(jnp.float32)
    part = total.astype(jnp.bfloat16)
    for s in range(64):
        out_ref[s] = part


def row_tiles(p):
    return 2 * (p ^ 4), 2 * (p ^ 4) + 1


def product_body(irrep_ref, mine_ref, other_ref, tiles_ref, out_ref, level_ref, held, slab, prod, code, in_sems, out_sems):
    def fetch(t):
        span = pl.ds(t * 5, 5)
        return pltpu.make_async_copy(tiles_ref.at[span], held.at[span], in_sems.at[t])

    def store(t):
        return pltpu.make_async_copy(code.at[t], out_ref.at[t], out_sems.at[t])

    for t in range(16):
        fetch(t).start()
    core = lax.axis_index("pair") % 2
    for source, shift in ((mine_ref, core), (other_ref, 1 - core)):
        for c in range(16):
            for x in range(4):
                rows = pl.ds(pl.multiple_of((2 * x + shift) * 16, 16), 16)
                slab[c // 2, rows, (c % 2) * 256 : (c % 2) * 256 + 256] = source[c * 4 + x]

    def multiply(step, top):
        for t in range(GROUP):
            fetch(step * GROUP + t).wait()
        count = GROUP * 5
        values = []
        for k in range(count + 1):
            if k < count:
                slot = step * count + k
                left = slab[jnp.maximum(irrep_ref[slot], 0)]
                right = held[slot].reshape(512, 128)
                values.append(jnp.dot(left, right, preferred_element_type=jnp.float32))
            if k > 0:
                slot = step * count + k - 1
                value = values[k - 1]
                prod[slot] = value
                high = jnp.max(jnp.abs(value).reshape(16, 8, 128), axis=0)
                top = jnp.maximum(top, jnp.where(irrep_ref[slot] >= 0, high, 0.0))
        return top

    top = lax.fori_loop(0, 16 // GROUP, multiply, jnp.zeros((8, 128), jnp.float32))
    top = jnp.max(jnp.max(top, axis=1, keepdims=True), axis=0, keepdims=True)
    level = jnp.ceil(jnp.log(jnp.maximum(top, 1e-30)) * (STEPS / LN2))
    level = jnp.broadcast_to(level, (8, 128))
    level_ref[...] = level.astype(jnp.int32)
    inverse = jnp.exp(level * (-LN2 / STEPS)) * TOP

    def quantise(t, carry):
        for k in range(5):
            value = prod[t * 5 + k]
            words = []
            for p in range(8):
                high, low = (
                    jnp.floor(value[u * 8 : u * 8 + 8, :] * inverse + 0.5).astype(jnp.int32) for u in row_tiles(p)
                )
                words.append((high << 16) | (low & 0xFFFF))
            for p in range(8):
                code[t, p, k] = words[p]
        store(t).start()
        return carry

    lax.fori_loop(0, 16, quantise, 0)
    for t in range(16):
        store(t).wait()


def select_body(from_ref, in_ref, level_ref, out_ref, picked, sems):
    def store(c):
        span = pl.ds(c * 4, 4)
        return pltpu.make_async_copy(picked.at[span], out_ref.at[span], sems.at[c])

    def one(t, carry):
        for i in range(16):
            picked[t, i] = in_ref[from_ref[t * 16 + i]]
        picked[t, 16] = level_ref[...]
        return carry

    for c in range(4):
        lax.fori_loop(c * 4, c * 4 + 4, one, 0)
        store(c).start()
    for c in range(4):
        store(c).wait()


def combine_body(own_ref, face_ref, here_ref, there_ref, pick_ref, sign_ref, out_ref, scale, result, sems):
    levels = jnp.concatenate([there_ref[s * 17 + 16] for s in range(16)], axis=0)
    pick = pick_ref[...]
    upper = jnp.dot(pick, (levels >> 5).astype(jnp.bfloat16), preferred_element_type=jnp.float32)
    lower = jnp.dot(pick, (levels & 31).astype(jnp.bfloat16), preferred_element_type=jnp.float32)
    scale[...] = jnp.exp((upper * 32.0 + lower) * (LN2 / STEPS)) * (1.0 / TOP) * sign_ref[...]

    def store(c):
        span = pl.ds(c * 8192, 8192)
        return pltpu.make_async_copy(result.at[:, span], out_ref.at[:, span], sems.at[c])

    def parts(word):
        return (word >> 16).astype(jnp.float32), ((word << 16) >> 16).astype(jnp.float32)

    def one(step, carry):
        rows = pl.multiple_of(step * 8, 8)
        own_scale = scale[pl.ds(rows, 8), :]
        face_scale = scale[pl.ds(256 + rows, 8), :]
        values = []
        for i in range(8):
            own = parts(here_ref[own_ref[step * 8 + i]])
            face = parts(there_ref[face_ref[step * 8 + i]])
            halves = [o * own_scale[i : i + 1, :] + f * face_scale[i : i + 1, :] for o, f in zip(own, face)]
            values.append(jnp.concatenate(halves, axis=0).astype(jnp.bfloat16))
        for i in range(8):
            result[:, pl.ds(pl.multiple_of((step * 8 + i) * 128, 128), 128)] = values[i]
        return carry

    for c in range(4):
        lax.fori_loop(c * 8, c * 8 + 8, one, 0)
        store(c).start()
    for c in range(4):
        store(c).wait()


def call_product(irreps, mine, other, tiles):
    dma = pltpu.SemaphoreType.DMA
    int32 = jnp.int32
    return call(
        product_body, [SMEM, VMEM, VMEM, HBM], [HBM, VMEM],
        [pltpu.HBM((16, 8, 5, 8, 128), int32), jax.ShapeDtypeStruct((8, 128), int32)],
        [
            pltpu.VMEM((80, 4, 128, 128), jnp.bfloat16),
            pltpu.VMEM((8, 128, 512), jnp.bfloat16),
            pltpu.VMEM((80, 128, 128), jnp.float32),
            pltpu.VMEM((16, 8, 5, 8, 128), int32),
            dma((16,)),
            dma((16,)),
        ],
        52 * MIB, 1_342_177_280, 14 << 20,
    )(irreps, mine, other, tiles)


def call_combine(own, face, here, there, pick, signs):
    scratch = [
        pltpu.VMEM((512, 128), jnp.float32),
        pltpu.VMEM((16, 32768), jnp.bfloat16),
        pltpu.SemaphoreType.DMA((4,)),
    ]
    out = jax.ShapeDtypeStruct((16, 32768), jnp.bfloat16)
    return call(combine_body, [SMEM] * 2 + [VMEM] * 4, HBM, out, scratch, 16 * MIB, 0, 4 << 20)(
        own, face, here, there, pick, signs
    )


def swap(value, mask):
    return lax.ppermute(value, "pair", [(i, i ^ mask) for i in range(8)])


def local(amplitudes, integrals, block_irrep, slab_blocks, owner, partner, sign):
    blk = lax.axis_index("blk")
    pair = lax.axis_index("pair")
    me = blk * 8 + pair
    int32 = jnp.int32
    dma = pltpu.SemaphoreType.DMA

    parts = call(
        extract_body, [SMEM, HBM], VMEM, jax.ShapeDtypeStruct((16, 16, 256), jnp.bfloat16), [dma((32,))], 60 * MIB, 0, 1 << 18
    )(slab_blocks, amplitudes)
    parts = lax.all_to_all(parts, "blk", split_axis=0, concat_axis=0, tiled=True)
    copies = call(
        merge_body, [VMEM], VMEM, jax.ShapeDtypeStruct((64, 16, 256), jnp.bfloat16), [], 4 * MIB, 0, 1 << 20
    )(parts)
    groups = [[c + 2 * i for i in range(64)] for c in range(2)]
    mine = lax.all_to_all(copies, BOTH, split_axis=0, concat_axis=0, tiled=True, axis_index_groups=groups)
    other = swap(mine, 1)

    ids = jnp.arange(256, dtype=int32)
    stored = (owner == me).reshape(16, 256)
    earlier = (ids[:, None] < ids[None, :]).astype(jnp.bfloat16)
    slot_rank = jnp.dot(stored.astype(jnp.bfloat16), earlier, preferred_element_type=jnp.float32).astype(int32)
    labels = block_irrep.reshape(16, 256) + 1
    chosen = stored[:, None, :] & (slot_rank[:, None, :] == jnp.arange(5, dtype=int32)[None, :, None])
    slot_irrep = (jnp.sum(jnp.where(chosen, labels[:, None, :], 0), axis=2) - 1).reshape(80)

    my_owner = lax.dynamic_slice_in_dim(owner, blk * 256, 256)
    my_partner = lax.dynamic_slice_in_dim(partner, blk * 256, 256)
    my_sign = lax.dynamic_slice_in_dim(sign, blk * 256, 256)
    before = ids[None, :] < ids[:, None]
    rank = jnp.sum((my_owner[None, :] == my_owner[:, None]) & before, axis=1).astype(int32)
    arrive = my_owner * 5 + rank
    leave_key = (my_partner // 256) * 256 + ids
    leave = jnp.sum(leave_key[None, :] < leave_key[:, None], axis=1).astype(int32)
    leaving = jnp.sum(jnp.where(leave[None, :] == ids[:, None], arrive[None, :], 0), axis=1).astype(int32)
    back = jnp.sum(my_partner[None, :] < my_partner[:, None], axis=1).astype(int32)
    all_ids = jnp.arange(4096, dtype=int32)
    face_owner = jnp.sum(jnp.where(my_partner[:, None] == all_ids[None, :], owner[None, :], 0), axis=1)
    back = back + back // 16
    rows = jnp.concatenate([my_owner ^ pair, face_owner ^ pair])
    pick = (rows[:, None] == jnp.arange(128, dtype=int32)[None, :]).astype(jnp.bfloat16)
    signs = jnp.concatenate([jnp.ones_like(my_sign), my_sign]).astype(jnp.float32)
    signs = jnp.broadcast_to(signs[:, None], (512, 128))

    coded, level = call_product(slot_irrep, mine, other, integrals)
    arrived = lax.all_to_all(coded.reshape(128, 40, 128), BOTH, split_axis=0, concat_axis=0, tiled=True)
    arrived = arrived.reshape(640, 8, 128)
    levels = level[:1]
    for mask in (1, 2, 4):
        levels = jnp.concatenate([levels, swap(levels, mask)], axis=0)
    outgoing = call(
        select_body, [SMEM, VMEM, VMEM], HBM, pltpu.HBM((16, 17, 8, 128), int32),
        [pltpu.VMEM((16, 17, 8, 128), int32), dma((4,))], 16 * MIB, 0, 3 << 20,
    )(leaving, arrived, levels)
    own = swap(outgoing, 4).reshape(272, 8, 128)
    incoming = lax.all_to_all(outgoing, "blk", split_axis=0, concat_axis=0, tiled=True).reshape(272, 8, 128)
    return call_combine(leave + leave // 16, back, own, incoming, pick, signs)


def solution(mesh):
    placed = (P("pair", "blk"), P(BOTH, None, None, None), P(), P(), P(), P(), P())
    return jax.shard_map(local, mesh=mesh, in_specs=placed, out_specs=P("pair", "blk"), check_vma=False)
```

```python
import jax
import jax.numpy as jnp
from jax import lax
from jax.experimental import pallas as pl
from jax.experimental.pallas import tpu as pltpu
from jax.sharding import PartitionSpec as P

BOTH = ("blk", "pair")
TOP = 32760.0
STEPS = 64.0
LN2 = 0.6931471805599453
MIB = 1 << 20
GROUP = 4
VMEM = pl.BlockSpec(memory_space=pltpu.VMEM)
HBM = pl.BlockSpec(memory_space=pltpu.HBM)
SMEM = pl.BlockSpec(memory_space=pltpu.SMEM)


def call(body, ins, outs, shapes, scratch, vmem, flops, moved):
    return pl.pallas_call(
        body,
        in_specs=ins,
        out_specs=outs,
        out_shape=shapes,
        scratch_shapes=scratch,
        compiler_params=pltpu.CompilerParams(vmem_limit_bytes=vmem),
        cost_estimate=pl.CostEstimate(flops=flops, bytes_accessed=moved, transcendentals=0),
    )


def extract_body(blocks_ref, amp_ref, out_ref, sems):
    blk = lax.axis_index("blk")

    def move(n):
        start = pl.multiple_of((blocks_ref[n] & 255) * 128, 128)
        return pltpu.make_async_copy(
            amp_ref.at[:, pl.ds(start, 128)],
            out_ref.at[n // 2, :, pl.ds((n % 2) * 128, 128)],
            sems.at[n],
        )

    for n in range(32):
        held = (blocks_ref[n] >> 8) == blk

        @pl.when(held)
        def _():
            move(n).start()

        @pl.when(jnp.logical_not(held))
        def _():
            out_ref[n // 2, :, (n % 2) * 128 : (n % 2) * 128 + 128] = jnp.zeros((16, 128), jnp.bfloat16)

    for n in range(32):

        @pl.when((blocks_ref[n] >> 8) == blk)
        def _():
            move(n).wait()


def merge_body(in_ref, out_ref):
    total = in_ref[0].astype(jnp.float32)
    for s in range(1, 16):
        total += in_ref[s].astype(jnp.float32)
    part = total.astype(jnp.bfloat16)
    for s in range(64):
        out_ref[s] = part


def row_tiles(p):
    return 2 * (p ^ 4), 2 * (p ^ 4) + 1


def product_body(irrep_ref, mine_ref, other_ref, tiles_ref, out_ref, level_ref, held, slab, prod, code, in_sems, out_sems):
    def fetch(t):
        span = pl.ds(t * 5, 5)
        return pltpu.make_async_copy(tiles_ref.at[span], held.at[span], in_sems.at[t])

    def store(t):
        return pltpu.make_async_copy(code.at[t], out_ref.at[t], out_sems.at[t])

    for t in range(16):
        fetch(t).start()
    core = lax.axis_index("pair") % 2
    for source, shift in ((mine_ref, core), (other_ref, 1 - core)):
        for c in range(16):
            for x in range(4):
                rows = pl.ds(pl.multiple_of((2 * x + shift) * 16, 16), 16)
                slab[c // 2, rows, (c % 2) * 256 : (c % 2) * 256 + 256] = source[c * 4 + x]

    def multiply(step, top):
        for t in range(GROUP):
            fetch(step * GROUP + t).wait()
        count = GROUP * 5
        values = []
        for k in range(count + 1):
            if k < count:
                slot = step * count + k
                left = slab[jnp.maximum(irrep_ref[slot], 0)]
                right = held[slot].reshape(512, 128)
                values.append(jnp.dot(left, right, preferred_element_type=jnp.float32))
            if k > 0:
                slot = step * count + k - 1
                value = values[k - 1]
                prod[slot] = value
                high = jnp.max(jnp.abs(value).reshape(16, 8, 128), axis=0)
                top = jnp.maximum(top, jnp.where(irrep_ref[slot] >= 0, high, 0.0))
        return top

    top = lax.fori_loop(0, 16 // GROUP, multiply, jnp.zeros((8, 128), jnp.float32))
    top = jnp.max(jnp.max(top, axis=1, keepdims=True), axis=0, keepdims=True)
    level = jnp.ceil(jnp.log(jnp.maximum(top, 1e-30)) * (STEPS / LN2))
    level = jnp.broadcast_to(level, (8, 128))
    level_ref[...] = level.astype(jnp.int32)
    inverse = jnp.exp(level * (-LN2 / STEPS)) * TOP

    def quantise(t, carry):
        for k in range(5):
            value = prod[t * 5 + k]
            words = []
            for p in range(8):
                high, low = (
                    jnp.floor(value[u * 8 : u * 8 + 8, :] * inverse + 0.5).astype(jnp.int32) for u in row_tiles(p)
                )
                words.append((high << 16) | (low & 0xFFFF))
            for p in range(8):
                code[t, p, k] = words[p]
        store(t).start()
        return carry

    lax.fori_loop(0, 16, quantise, 0)
    for t in range(16):
        store(t).wait()


def select_body(from_ref, in_ref, level_ref, out_ref, words_ref, picked, sems, word_sems):
    def store(c):
        span = pl.ds(c * 4, 4)
        return pltpu.make_async_copy(picked.at[span], out_ref.at[span], sems.at[c])

    def store_words(c):
        span = pl.ds(c * 4, 4)
        return pltpu.make_async_copy(picked.at[span, pl.ds(0, 16)], words_ref.at[span], word_sems.at[c])

    def one(t, carry):
        for i in range(16):
            picked[t, i] = in_ref[from_ref[t * 16 + i]]
        picked[t, 16] = level_ref[...]
        return carry

    for c in range(4):
        lax.fori_loop(c * 4, c * 4 + 4, one, 0)
        store_words(c).start()
        store(c).start()
    for c in range(4):
        store_words(c).wait()
        store(c).wait()


def combine_body(own_ref, face_ref, here_ref, there_ref, pick_ref, sign_ref, out_ref, scale, result, sems):
    levels = jnp.concatenate([there_ref[s * 17 + 16] for s in range(16)], axis=0)
    pick = pick_ref[...]
    upper = jnp.dot(pick, (levels >> 5).astype(jnp.bfloat16), preferred_element_type=jnp.float32)
    lower = jnp.dot(pick, (levels & 31).astype(jnp.bfloat16), preferred_element_type=jnp.float32)
    scale[...] = jnp.exp((upper * 32.0 + lower) * (LN2 / STEPS)) * (1.0 / TOP) * sign_ref[...]

    def store(c):
        span = pl.ds(c * 8192, 8192)
        return pltpu.make_async_copy(result.at[:, span], out_ref.at[:, span], sems.at[c])

    def parts(word):
        return (word >> 16).astype(jnp.float32), ((word << 16) >> 16).astype(jnp.float32)

    def one(step, carry):
        rows = pl.multiple_of(step * 8, 8)
        own_scale = scale[pl.ds(rows, 8), :]
        face_scale = scale[pl.ds(256 + rows, 8), :]
        values = []
        for i in range(8):
            own = parts(here_ref[own_ref[step * 8 + i]])
            face = parts(there_ref[face_ref[step * 8 + i]])
            halves = [o * own_scale[i : i + 1, :] + f * face_scale[i : i + 1, :] for o, f in zip(own, face)]
            values.append(jnp.concatenate(halves, axis=0).astype(jnp.bfloat16))
        for i in range(8):
            result[:, pl.ds(pl.multiple_of((step * 8 + i) * 128, 128), 128)] = values[i]
        return carry

    for c in range(4):
        lax.fori_loop(c * 8, c * 8 + 8, one, 0)
        store(c).start()
    for c in range(4):
        store(c).wait()


def call_product(irreps, mine, other, tiles):
    dma = pltpu.SemaphoreType.DMA
    int32 = jnp.int32
    return call(
        product_body, [SMEM, VMEM, VMEM, HBM], [HBM, VMEM],
        [pltpu.HBM((16, 8, 5, 8, 128), int32), jax.ShapeDtypeStruct((8, 128), int32)],
        [
            pltpu.VMEM((80, 4, 128, 128), jnp.bfloat16),
            pltpu.VMEM((8, 128, 512), jnp.bfloat16),
            pltpu.VMEM((80, 128, 128), jnp.float32),
            pltpu.VMEM((16, 8, 5, 8, 128), int32),
            dma((16,)),
            dma((16,)),
        ],
        52 * MIB, 1_342_177_280, 14 << 20,
    )(irreps, mine, other, tiles)


def call_combine(own, face, here, there, pick, signs):
    scratch = [
        pltpu.VMEM((512, 128), jnp.float32),
        pltpu.VMEM((16, 32768), jnp.bfloat16),
        pltpu.SemaphoreType.DMA((4,)),
    ]
    out = jax.ShapeDtypeStruct((16, 32768), jnp.bfloat16)
    return call(combine_body, [SMEM] * 2 + [VMEM] * 4, HBM, out, scratch, 16 * MIB, 0, 4 << 20)(
        own, face, here, there, pick, signs
    )


def swap(value, mask):
    return lax.ppermute(value, "pair", [(i, i ^ mask) for i in range(8)])


def local(amplitudes, integrals, block_irrep, slab_blocks, owner, partner, sign):
    blk = lax.axis_index("blk")
    pair = lax.axis_index("pair")
    me = blk * 8 + pair
    int32 = jnp.int32
    dma = pltpu.SemaphoreType.DMA

    parts = call(
        extract_body, [SMEM, HBM], VMEM, jax.ShapeDtypeStruct((16, 16, 256), jnp.bfloat16), [dma((32,))], 60 * MIB, 0, 1 << 18
    )(slab_blocks, amplitudes)
    parts = lax.all_to_all(parts, "blk", split_axis=0, concat_axis=0, tiled=True)
    copies = call(
        merge_body, [VMEM], VMEM, jax.ShapeDtypeStruct((64, 16, 256), jnp.bfloat16), [], 4 * MIB, 0, 1 << 20
    )(parts)
    groups = [[c + 2 * i for i in range(64)] for c in range(2)]
    mine = lax.all_to_all(copies, BOTH, split_axis=0, concat_axis=0, tiled=True, axis_index_groups=groups)
    other = swap(mine, 1)

    ids = jnp.arange(256, dtype=int32)
    stored = (owner == me).reshape(16, 256)
    earlier = (ids[:, None] < ids[None, :]).astype(jnp.bfloat16)
    slot_rank = jnp.dot(stored.astype(jnp.bfloat16), earlier, preferred_element_type=jnp.float32).astype(int32)
    labels = block_irrep.reshape(16, 256) + 1
    chosen = stored[:, None, :] & (slot_rank[:, None, :] == jnp.arange(5, dtype=int32)[None, :, None])
    slot_irrep = (jnp.sum(jnp.where(chosen, labels[:, None, :], 0), axis=2) - 1).reshape(80)

    my_owner = lax.dynamic_slice_in_dim(owner, blk * 256, 256)
    my_partner = lax.dynamic_slice_in_dim(partner, blk * 256, 256)
    my_sign = lax.dynamic_slice_in_dim(sign, blk * 256, 256)
    before = ids[None, :] < ids[:, None]
    rank = jnp.sum((my_owner[None, :] == my_owner[:, None]) & before, axis=1).astype(int32)
    arrive = my_owner * 5 + rank
    leave_key = (my_partner // 256) * 256 + ids
    leave = jnp.sum(leave_key[None, :] < leave_key[:, None], axis=1).astype(int32)
    leaving = jnp.sum(jnp.where(leave[None, :] == ids[:, None], arrive[None, :], 0), axis=1).astype(int32)
    back = jnp.sum(my_partner[None, :] < my_partner[:, None], axis=1).astype(int32)
    all_ids = jnp.arange(4096, dtype=int32)
    face_owner = jnp.sum(jnp.where(my_partner[:, None] == all_ids[None, :], owner[None, :], 0), axis=1)
    back = back + back // 16
    rows = jnp.concatenate([my_owner ^ pair, face_owner ^ pair])
    pick = (rows[:, None] == jnp.arange(128, dtype=int32)[None, :]).astype(jnp.bfloat16)
    signs = jnp.concatenate([jnp.ones_like(my_sign), my_sign]).astype(jnp.float32)
    signs = jnp.broadcast_to(signs[:, None], (512, 128))

    coded, level = call_product(slot_irrep, mine, other, integrals)
    arrived = lax.all_to_all(coded.reshape(128, 40, 128), BOTH, split_axis=0, concat_axis=0, tiled=True)
    arrived = arrived.reshape(640, 8, 128)
    levels = level[:1]
    for mask in (1, 2, 4):
        levels = jnp.concatenate([levels, swap(levels, mask)], axis=0)
    outgoing, words = call(
        select_body, [SMEM, VMEM, VMEM], [HBM, HBM],
        [pltpu.HBM((16, 17, 8, 128), int32), pltpu.HBM((16, 16, 8, 128), int32)],
        [pltpu.VMEM((16, 17, 8, 128), int32), dma((4,)), dma((4,))], 16 * MIB, 0, 4 << 20,
    )(leaving, arrived, levels)
    own = swap(words, 4).reshape(256, 8, 128)
    incoming = lax.all_to_all(outgoing, "blk", split_axis=0, concat_axis=0, tiled=True).reshape(272, 8, 128)
    return call_combine(leave, back, own, incoming, pick, signs)


def solution(mesh):
    placed = (P("pair", "blk"), P(BOTH, None, None, None), P(), P(), P(), P(), P())
    return jax.shard_map(local, mesh=mesh, in_specs=placed, out_specs=P("pair", "blk"), check_vma=False)
```

```python
import jax
import jax.numpy as jnp
from jax import lax
from jax.experimental import pallas as pl
from jax.experimental.pallas import tpu as pltpu
from jax.sharding import PartitionSpec as P

BOTH = ("blk", "pair")
TOP = 32760.0
STEPS = 64.0
LN2 = 0.6931471805599453
MIB = 1 << 20
GROUP = 4
VMEM = pl.BlockSpec(memory_space=pltpu.VMEM)
HBM = pl.BlockSpec(memory_space=pltpu.HBM)
SMEM = pl.BlockSpec(memory_space=pltpu.SMEM)


def call(body, ins, outs, shapes, scratch, vmem, flops, moved):
    return pl.pallas_call(
        body,
        in_specs=ins,
        out_specs=outs,
        out_shape=shapes,
        scratch_shapes=scratch,
        compiler_params=pltpu.CompilerParams(vmem_limit_bytes=vmem),
        cost_estimate=pl.CostEstimate(flops=flops, bytes_accessed=moved, transcendentals=0),
    )


def extract_body(blocks_ref, amp_ref, out_ref):
    blk = lax.axis_index("blk")
    for c in range(16):
        tiles = []
        for n in (2 * c, 2 * c + 1):
            block = blocks_ref[n]
            tile = amp_ref[:, pl.ds(pl.multiple_of((block & 255) * 128, 128), 128)]
            tiles.append(jnp.where((block >> 8) == blk, tile, jnp.zeros_like(tile)))
        out_ref[c] = jnp.concatenate(tiles, axis=1)


def merge_body(in_ref, out_ref):
    total = in_ref[0].astype(jnp.float32)
    for s in range(1, 16):
        total += in_ref[s].astype(jnp.float32)
    part = total.astype(jnp.bfloat16)
    for s in range(64):
        out_ref[s] = part


def row_tiles(p):
    return 2 * (p ^ 4), 2 * (p ^ 4) + 1


def product_body(irrep_ref, mine_ref, other_ref, tiles_ref, out_ref, level_ref, held, slab, prod, code, in_sems, out_sems):
    def fetch(t):
        span = pl.ds(t * 5, 5)
        return pltpu.make_async_copy(tiles_ref.at[span], held.at[span], in_sems.at[t])

    def store(t):
        return pltpu.make_async_copy(code.at[t], out_ref.at[t], out_sems.at[t])

    for t in range(16):
        fetch(t).start()
    core = lax.axis_index("pair") % 2
    for source, shift in ((mine_ref, core), (other_ref, 1 - core)):
        for c in range(16):
            for x in range(4):
                rows = pl.ds(pl.multiple_of((2 * x + shift) * 16, 16), 16)
                slab[c // 2, rows, (c % 2) * 256 : (c % 2) * 256 + 256] = source[c * 4 + x]

    def multiply(step, top):
        for t in range(GROUP):
            fetch(step * GROUP + t).wait()
        count = GROUP * 5
        values = []
        for k in range(count + 1):
            if k < count:
                slot = step * count + k
                left = slab[jnp.maximum(irrep_ref[slot], 0)]
                right = held[slot].reshape(512, 128)
                values.append(jnp.dot(left, right, preferred_element_type=jnp.float32))
            if k > 0:
                slot = step * count + k - 1
                value = values[k - 1]
                prod[slot] = value
                high = jnp.max(jnp.abs(value).reshape(16, 8, 128), axis=0)
                top = jnp.maximum(top, jnp.where(irrep_ref[slot] >= 0, high, 0.0))
        return top

    top = lax.fori_loop(0, 16 // GROUP, multiply, jnp.zeros((8, 128), jnp.float32))
    top = jnp.max(jnp.max(top, axis=1, keepdims=True), axis=0, keepdims=True)
    level = jnp.ceil(jnp.log(jnp.maximum(top, 1e-30)) * (STEPS / LN2))
    level = jnp.broadcast_to(level, (8, 128))
    level_ref[...] = level.astype(jnp.int32)
    inverse = jnp.exp(level * (-LN2 / STEPS)) * TOP

    def quantise(t, carry):
        for k in range(5):
            value = prod[t * 5 + k]
            words = []
            for p in range(8):
                high, low = (
                    jnp.floor(value[u * 8 : u * 8 + 8, :] * inverse + 0.5).astype(jnp.int32) for u in row_tiles(p)
                )
                words.append((high << 16) | (low & 0xFFFF))
            for p in range(8):
                code[t, p, k] = words[p]
        store(t).start()
        return carry

    lax.fori_loop(0, 16, quantise, 0)
    for t in range(16):
        store(t).wait()


def select_body(from_ref, in_ref, level_ref, out_ref, words_ref, picked, sems, word_sems):
    def store(c):
        span = pl.ds(c * 2, 2)
        return pltpu.make_async_copy(picked.at[span], out_ref.at[span], sems.at[c])

    def store_words(c):
        span = pl.ds(c * 2, 2)
        return pltpu.make_async_copy(picked.at[span, pl.ds(0, 16)], words_ref.at[span], word_sems.at[c])

    def one(t, carry):
        for i in range(16):
            picked[t, i] = in_ref[from_ref[t * 16 + i]]
        picked[t, 16] = level_ref[...]
        return carry

    for c in range(8):
        lax.fori_loop(c * 2, c * 2 + 2, one, 0)
        store_words(c).start()
        store(c).start()
    for c in range(8):
        store_words(c).wait()
        store(c).wait()


def combine_body(own_ref, face_ref, here_ref, there_ref, pick_ref, sign_ref, out_ref, scale, result, sems):
    levels = jnp.concatenate([there_ref[s * 17 + 16] for s in range(16)], axis=0)
    pick = pick_ref[...]
    upper = jnp.dot(pick, (levels >> 5).astype(jnp.bfloat16), preferred_element_type=jnp.float32)
    lower = jnp.dot(pick, (levels & 31).astype(jnp.bfloat16), preferred_element_type=jnp.float32)
    value = jnp.exp((upper * 32.0 + lower) * (LN2 / STEPS)) * (1.0 / TOP)
    scale[:256] = value[:256]
    scale[256:] = value[256:] * sign_ref[...]

    def store(c):
        span = pl.ds(c * 4096, 4096)
        return pltpu.make_async_copy(result.at[:, span], out_ref.at[:, span], sems.at[c])

    def parts(word):
        return (word >> 16).astype(jnp.float32), ((word << 16) >> 16).astype(jnp.float32)

    def one(step, carry):
        rows = pl.multiple_of(step * 8, 8)
        own_scale = scale[pl.ds(rows, 8), :]
        face_scale = scale[pl.ds(256 + rows, 8), :]
        values = []
        for i in range(8):
            own = parts(here_ref[own_ref[step * 8 + i]])
            face = parts(there_ref[face_ref[step * 8 + i]])
            halves = [o * own_scale[i : i + 1, :] + f * face_scale[i : i + 1, :] for o, f in zip(own, face)]
            values.append(jnp.concatenate(halves, axis=0).astype(jnp.bfloat16))
        for i in range(8):
            result[:, pl.ds(pl.multiple_of((step * 8 + i) * 128, 128), 128)] = values[i]
        return carry

    for c in range(8):
        lax.fori_loop(c * 4, c * 4 + 4, one, 0)
        store(c).start()
    for c in range(8):
        store(c).wait()


def call_product(irreps, mine, other, tiles):
    dma = pltpu.SemaphoreType.DMA
    int32 = jnp.int32
    return call(
        product_body, [SMEM, VMEM, VMEM, HBM], [HBM, VMEM],
        [pltpu.HBM((16, 8, 5, 8, 128), int32), jax.ShapeDtypeStruct((8, 128), int32)],
        [
            pltpu.VMEM((80, 4, 128, 128), jnp.bfloat16),
            pltpu.VMEM((8, 128, 512), jnp.bfloat16),
            pltpu.VMEM((80, 128, 128), jnp.float32),
            pltpu.VMEM((16, 8, 5, 8, 128), int32),
            dma((16,)),
            dma((16,)),
        ],
        52 * MIB, 1_342_177_280, 14 << 20,
    )(irreps, mine, other, tiles)


def call_combine(own, face, here, there, pick, signs):
    scratch = [
        pltpu.VMEM((512, 128), jnp.float32),
        pltpu.VMEM((16, 32768), jnp.bfloat16),
        pltpu.SemaphoreType.DMA((8,)),
    ]
    out = jax.ShapeDtypeStruct((16, 32768), jnp.bfloat16)
    return call(combine_body, [SMEM] * 2 + [VMEM] * 4, HBM, out, scratch, 16 * MIB, 0, 4 << 20)(
        own, face, here, there, pick, signs
    )


def swap(value, mask):
    return lax.ppermute(value, "pair", [(i, i ^ mask) for i in range(8)])


def local(amplitudes, integrals, block_irrep, slab_blocks, owner, partner, sign):
    blk = lax.axis_index("blk")
    pair = lax.axis_index("pair")
    me = blk * 8 + pair
    int32 = jnp.int32
    dma = pltpu.SemaphoreType.DMA

    parts = call(
        extract_body, [SMEM, VMEM], VMEM, jax.ShapeDtypeStruct((16, 16, 256), jnp.bfloat16), [], 4 * MIB, 0, 1 << 20
    )(slab_blocks, amplitudes)
    parts = lax.all_to_all(parts, "blk", split_axis=0, concat_axis=0, tiled=True)
    copies = call(
        merge_body, [VMEM], VMEM, jax.ShapeDtypeStruct((64, 16, 256), jnp.bfloat16), [], 4 * MIB, 0, 1 << 20
    )(parts)
    groups = [[c + 2 * i for i in range(64)] for c in range(2)]
    mine = lax.all_to_all(copies, BOTH, split_axis=0, concat_axis=0, tiled=True, axis_index_groups=groups)
    other = swap(mine, 1)

    ids = jnp.arange(256, dtype=int32)
    stored = (owner == me).reshape(16, 256)
    earlier = (ids[:, None] < ids[None, :]).astype(jnp.bfloat16)
    slot_rank = jnp.dot(stored.astype(jnp.bfloat16), earlier, preferred_element_type=jnp.float32).astype(int32)
    labels = block_irrep.reshape(16, 256) + 1
    chosen = stored[:, None, :] & (slot_rank[:, None, :] == jnp.arange(5, dtype=int32)[None, :, None])
    slot_irrep = (jnp.sum(jnp.where(chosen, labels[:, None, :], 0), axis=2) - 1).reshape(80)

    my_owner = lax.dynamic_slice_in_dim(owner, blk * 256, 256)
    my_partner = lax.dynamic_slice_in_dim(partner, blk * 256, 256)
    my_sign = lax.dynamic_slice_in_dim(sign, blk * 256, 256)
    before = ids[None, :] < ids[:, None]
    rank = jnp.sum((my_owner[None, :] == my_owner[:, None]) & before, axis=1).astype(int32)
    arrive = my_owner * 5 + rank
    leave_key = (my_partner // 256) * 256 + ids
    leave = jnp.sum(leave_key[None, :] < leave_key[:, None], axis=1).astype(int32)
    leaving = jnp.sum(jnp.where(leave[None, :] == ids[:, None], arrive[None, :], 0), axis=1).astype(int32)
    back = jnp.sum(my_partner[None, :] < my_partner[:, None], axis=1).astype(int32)
    all_ids = jnp.arange(4096, dtype=int32)
    face_owner = jnp.sum(jnp.where(my_partner[:, None] == all_ids[None, :], owner[None, :], 0), axis=1)
    back = back + back // 16
    rows = jnp.concatenate([my_owner ^ pair, face_owner ^ pair])
    pick = (rows[:, None] == jnp.arange(128, dtype=int32)[None, :]).astype(jnp.bfloat16)
    signs = jnp.broadcast_to(my_sign.astype(jnp.float32)[:, None], (256, 128))

    coded, level = call_product(slot_irrep, mine, other, integrals)
    arrived = lax.all_to_all(coded.reshape(128, 40, 128), BOTH, split_axis=0, concat_axis=0, tiled=True)
    arrived = arrived.reshape(640, 8, 128)
    levels = level[:1]
    for mask in (1, 2, 4):
        levels = jnp.concatenate([levels, swap(levels, mask)], axis=0)
    outgoing, words = call(
        select_body, [SMEM, VMEM, VMEM], [HBM, HBM],
        [pltpu.HBM((16, 17, 8, 128), int32), pltpu.HBM((16, 16, 8, 128), int32)],
        [pltpu.VMEM((16, 17, 8, 128), int32), dma((8,)), dma((8,))], 16 * MIB, 0, 4 << 20,
    )(leaving, arrived, levels)
    own = swap(words, 4).reshape(256, 8, 128)
    incoming = lax.all_to_all(outgoing, "blk", split_axis=0, concat_axis=0, tiled=True).reshape(272, 8, 128)
    return call_combine(leave, back, own, incoming, pick, signs)


def solution(mesh):
    placed = (P("pair", "blk"), P(BOTH, None, None, None), P(), P(), P(), P(), P())
    return jax.shard_map(local, mesh=mesh, in_specs=placed, out_specs=P("pair", "blk"), check_vma=False)
```

```python
import jax
import jax.numpy as jnp
from jax import lax
from jax.experimental import pallas as pl
from jax.experimental.pallas import tpu as pltpu
from jax.sharding import PartitionSpec as P

BOTH = ("blk", "pair")
TOP = 32760.0
STEPS = 64.0
LN2 = 0.6931471805599453
MIB = 1 << 20
GROUP = 4
VMEM = pl.BlockSpec(memory_space=pltpu.VMEM)
HBM = pl.BlockSpec(memory_space=pltpu.HBM)
SMEM = pl.BlockSpec(memory_space=pltpu.SMEM)


def call(body, ins, outs, shapes, scratch, vmem, flops, moved):
    return pl.pallas_call(
        body,
        in_specs=ins,
        out_specs=outs,
        out_shape=shapes,
        scratch_shapes=scratch,
        compiler_params=pltpu.CompilerParams(vmem_limit_bytes=vmem),
        cost_estimate=pl.CostEstimate(flops=flops, bytes_accessed=moved, transcendentals=0),
    )


def extract_body(blocks_ref, amp_ref, out_ref):
    blk = lax.axis_index("blk")
    for c in range(16):
        tiles = []
        for n in (2 * c, 2 * c + 1):
            block = blocks_ref[n]
            tile = amp_ref[:, pl.ds(pl.multiple_of((block & 255) * 128, 128), 128)]
            tiles.append(jnp.where((block >> 8) == blk, tile, jnp.zeros_like(tile)))
        out_ref[c] = jnp.concatenate(tiles, axis=1)


def merge_body(in_ref, out_ref):
    total = in_ref[0].astype(jnp.float32)
    for s in range(1, 16):
        total += in_ref[s].astype(jnp.float32)
    part = total.astype(jnp.bfloat16)
    for s in range(64):
        out_ref[s] = part


def row_tiles(p):
    return 2 * (p ^ 4), 2 * (p ^ 4) + 1


def product_body(irrep_ref, mine_ref, other_ref, tiles_ref, out_ref, level_ref, held, slab, prod, code, in_sems, out_sems):
    def fetch(t):
        span = pl.ds(t * 5, 5)
        return pltpu.make_async_copy(tiles_ref.at[span], held.at[span], in_sems.at[t])

    def store(t):
        return pltpu.make_async_copy(code.at[t], out_ref.at[t], out_sems.at[t])

    for t in range(16):
        fetch(t).start()
    core = lax.axis_index("pair") % 2
    for source, shift in ((mine_ref, core), (other_ref, 1 - core)):
        for c in range(16):
            for x in range(4):
                rows = pl.ds(pl.multiple_of((2 * x + shift) * 16, 16), 16)
                slab[c // 2, rows, (c % 2) * 256 : (c % 2) * 256 + 256] = source[c * 4 + x]

    def multiply(step, top):
        for t in range(GROUP):
            fetch(step * GROUP + t).wait()
        count = GROUP * 5
        values = []
        for k in range(count + 1):
            if k < count:
                slot = step * count + k
                left = slab[jnp.maximum(irrep_ref[slot], 0)]
                right = held[slot].reshape(512, 128)
                values.append(jnp.dot(left, right, preferred_element_type=jnp.float32))
            if k > 0:
                slot = step * count + k - 1
                value = values[k - 1]
                prod[slot] = value
                high = jnp.max(jnp.abs(value).reshape(16, 8, 128), axis=0)
                top = jnp.maximum(top, jnp.where(irrep_ref[slot] >= 0, high, 0.0))
        return top

    top = lax.fori_loop(0, 16 // GROUP, multiply, jnp.zeros((8, 128), jnp.float32))
    top = jnp.max(jnp.max(top, axis=1, keepdims=True), axis=0, keepdims=True)
    level = jnp.ceil(jnp.log(jnp.maximum(top, 1e-30)) * (STEPS / LN2))
    level = jnp.broadcast_to(level, (8, 128))
    level_ref[...] = level.astype(jnp.int32)
    inverse = jnp.exp(level * (-LN2 / STEPS)) * TOP

    def quantise(t, carry):
        for k in range(5):
            value = prod[t * 5 + k]
            words = []
            for p in range(8):
                high, low = (
                    jnp.floor(value[u * 8 : u * 8 + 8, :] * inverse + 0.5).astype(jnp.int32) for u in row_tiles(p)
                )
                words.append((high << 16) | (low & 0xFFFF))
            for p in range(8):
                code[t, p, k] = words[p]
        store(t).start()
        return carry

    lax.fori_loop(0, 16, quantise, 0)
    for t in range(16):
        store(t).wait()


def select_body(from_ref, in_ref, level_ref, out_ref, words_ref, picked, sems, word_sems):
    def store(c):
        span = pl.ds(c * 2, 2)
        return pltpu.make_async_copy(picked.at[span], out_ref.at[span], sems.at[c])

    def store_words(c):
        span = pl.ds(c * 2, 2)
        return pltpu.make_async_copy(picked.at[span, pl.ds(0, 16)], words_ref.at[span], word_sems.at[c])

    def one(t, carry):
        for i in range(16):
            picked[t, i] = in_ref[from_ref[t * 16 + i]]
        picked[t, 16] = level_ref[...]
        return carry

    for c in range(8):
        lax.fori_loop(c * 2, c * 2 + 2, one, 0)
        store_words(c).start()
        store(c).start()
    for c in range(8):
        store_words(c).wait()
        store(c).wait()


def combine_body(own_ref, face_ref, here_ref, there_ref, pick_ref, sign_ref, out_ref, scale, result, sems):
    levels = jnp.concatenate([there_ref[s * 17 + 16] for s in range(16)], axis=0)
    pick = pick_ref[...]
    upper = jnp.dot(pick, (levels >> 5).astype(jnp.bfloat16), preferred_element_type=jnp.float32)
    lower = jnp.dot(pick, (levels & 31).astype(jnp.bfloat16), preferred_element_type=jnp.float32)
    value = jnp.exp((upper * 32.0 + lower) * (LN2 / STEPS)) * (1.0 / TOP)
    scale[:256] = value[:256]
    scale[256:] = value[256:] * sign_ref[...]

    def store(c):
        span = pl.ds(c * 4096, 4096)
        return pltpu.make_async_copy(result.at[:, span], out_ref.at[:, span], sems.at[c])

    def parts(word):
        return (word >> 16).astype(jnp.float32), ((word << 16) >> 16).astype(jnp.float32)

    def one(step, carry):
        rows = pl.multiple_of(step * 8, 8)
        own_scale = scale[pl.ds(rows, 8), :]
        face_scale = scale[pl.ds(256 + rows, 8), :]
        values = []
        for i in range(8):
            own = parts(here_ref[own_ref[step * 8 + i]])
            face = parts(there_ref[face_ref[step * 8 + i]])
            halves = [o * own_scale[i : i + 1, :] + f * face_scale[i : i + 1, :] for o, f in zip(own, face)]
            values.append(jnp.concatenate(halves, axis=0).astype(jnp.bfloat16))
        for i in range(8):
            result[:, pl.ds(pl.multiple_of((step * 8 + i) * 128, 128), 128)] = values[i]
        return carry

    for c in range(8):
        lax.fori_loop(c * 4, c * 4 + 4, one, 0)
        store(c).start()
    for c in range(8):
        store(c).wait()


def call_product(irreps, mine, other, tiles):
    dma = pltpu.SemaphoreType.DMA
    int32 = jnp.int32
    return call(
        product_body, [SMEM, VMEM, VMEM, HBM], [HBM, VMEM],
        [pltpu.HBM((16, 8, 5, 8, 128), int32), jax.ShapeDtypeStruct((8, 128), int32)],
        [
            pltpu.VMEM((80, 4, 128, 128), jnp.bfloat16),
            pltpu.VMEM((8, 128, 512), jnp.bfloat16),
            pltpu.VMEM((80, 128, 128), jnp.float32),
            pltpu.VMEM((16, 8, 5, 8, 128), int32),
            dma((16,)),
            dma((16,)),
        ],
        52 * MIB, 1_342_177_280, 14 << 20,
    )(irreps, mine, other, tiles)


def call_combine(own, face, here, there, pick, signs):
    scratch = [
        pltpu.VMEM((512, 128), jnp.float32),
        pltpu.VMEM((16, 32768), jnp.bfloat16),
        pltpu.SemaphoreType.DMA((8,)),
    ]
    out = jax.ShapeDtypeStruct((16, 32768), jnp.bfloat16)
    return call(combine_body, [SMEM] * 2 + [VMEM] * 4, HBM, out, scratch, 16 * MIB, 0, 4 << 20)(
        own, face, here, there, pick, signs
    )


def swap(value, mask):
    return lax.ppermute(value, "pair", [(i, i ^ mask) for i in range(8)])


def local(amplitudes, integrals, block_irrep, slab_blocks, owner, partner, sign):
    blk = lax.axis_index("blk")
    pair = lax.axis_index("pair")
    me = blk * 8 + pair
    int32 = jnp.int32
    dma = pltpu.SemaphoreType.DMA

    parts = call(
        extract_body, [SMEM, VMEM], VMEM, jax.ShapeDtypeStruct((16, 16, 256), jnp.bfloat16), [], 53 * MIB, 0, 1 << 20
    )(slab_blocks, amplitudes)
    parts = lax.all_to_all(parts, "blk", split_axis=0, concat_axis=0, tiled=True)
    copies = call(
        merge_body, [VMEM], VMEM, jax.ShapeDtypeStruct((64, 16, 256), jnp.bfloat16), [], 4 * MIB, 0, 1 << 20
    )(parts)
    groups = [[c + 2 * i for i in range(64)] for c in range(2)]
    mine = lax.all_to_all(copies, BOTH, split_axis=0, concat_axis=0, tiled=True, axis_index_groups=groups)
    other = swap(mine, 1)

    ids = jnp.arange(256, dtype=int32)
    stored = (owner == me).reshape(16, 256)
    earlier = (ids[:, None] < ids[None, :]).astype(jnp.bfloat16)
    slot_rank = jnp.dot(stored.astype(jnp.bfloat16), earlier, preferred_element_type=jnp.float32).astype(int32)
    labels = block_irrep.reshape(16, 256) + 1
    chosen = stored[:, None, :] & (slot_rank[:, None, :] == jnp.arange(5, dtype=int32)[None, :, None])
    slot_irrep = (jnp.sum(jnp.where(chosen, labels[:, None, :], 0), axis=2) - 1).reshape(80)

    my_owner = lax.dynamic_slice_in_dim(owner, blk * 256, 256)
    my_partner = lax.dynamic_slice_in_dim(partner, blk * 256, 256)
    my_sign = lax.dynamic_slice_in_dim(sign, blk * 256, 256)
    before = ids[None, :] < ids[:, None]
    rank = jnp.sum((my_owner[None, :] == my_owner[:, None]) & before, axis=1).astype(int32)
    arrive = my_owner * 5 + rank
    leave_key = (my_partner // 256) * 256 + ids
    leave = jnp.sum(leave_key[None, :] < leave_key[:, None], axis=1).astype(int32)
    leaving = jnp.sum(jnp.where(leave[None, :] == ids[:, None], arrive[None, :], 0), axis=1).astype(int32)
    back = jnp.sum(my_partner[None, :] < my_partner[:, None], axis=1).astype(int32)
    all_ids = jnp.arange(4096, dtype=int32)
    face_owner = jnp.sum(jnp.where(my_partner[:, None] == all_ids[None, :], owner[None, :], 0), axis=1)
    back = back + back // 16
    rows = jnp.concatenate([my_owner ^ pair, face_owner ^ pair])
    pick = (rows[:, None] == jnp.arange(128, dtype=int32)[None, :]).astype(jnp.bfloat16)
    signs = jnp.broadcast_to(my_sign.astype(jnp.float32)[:, None], (256, 128))

    coded, level = call_product(slot_irrep, mine, other, integrals)
    arrived = lax.all_to_all(coded.reshape(128, 40, 128), BOTH, split_axis=0, concat_axis=0, tiled=True)
    arrived = arrived.reshape(640, 8, 128)
    levels = level[:1]
    for mask in (1, 2, 4):
        levels = jnp.concatenate([levels, swap(levels, mask)], axis=0)
    outgoing, words = call(
        select_body, [SMEM, VMEM, VMEM], [HBM, HBM],
        [pltpu.HBM((16, 17, 8, 128), int32), pltpu.HBM((16, 16, 8, 128), int32)],
        [pltpu.VMEM((16, 17, 8, 128), int32), dma((8,)), dma((8,))], 16 * MIB, 0, 4 << 20,
    )(leaving, arrived, levels)
    own = swap(words, 4).reshape(256, 8, 128)
    incoming = lax.all_to_all(outgoing, "blk", split_axis=0, concat_axis=0, tiled=True).reshape(272, 8, 128)
    return call_combine(leave, back, own, incoming, pick, signs)


def solution(mesh):
    placed = (P("pair", "blk"), P(BOTH, None, None, None), P(), P(), P(), P(), P())
    return jax.shard_map(local, mesh=mesh, in_specs=placed, out_specs=P("pair", "blk"), check_vma=False)
```

```python
import jax
import jax.numpy as jnp
from jax import lax
from jax.experimental import pallas as pl
from jax.experimental.pallas import tpu as pltpu
from jax.sharding import PartitionSpec as P

BOTH = ("blk", "pair")
TOP = 32760.0
STEPS = 64.0
LN2 = 0.6931471805599453
MIB = 1 << 20
GROUP = 4
VMEM = pl.BlockSpec(memory_space=pltpu.VMEM)
HBM = pl.BlockSpec(memory_space=pltpu.HBM)
SMEM = pl.BlockSpec(memory_space=pltpu.SMEM)


def call(body, ins, outs, shapes, scratch, vmem, flops, moved):
    return pl.pallas_call(
        body,
        in_specs=ins,
        out_specs=outs,
        out_shape=shapes,
        scratch_shapes=scratch,
        compiler_params=pltpu.CompilerParams(vmem_limit_bytes=vmem),
        cost_estimate=pl.CostEstimate(flops=flops, bytes_accessed=moved, transcendentals=0),
    )


def extract_body(blocks_ref, amp_ref, out_ref):
    blk = lax.axis_index("blk")
    for c in range(16):
        tiles = []
        for n in (2 * c, 2 * c + 1):
            block = blocks_ref[n]
            tile = amp_ref[:, pl.ds(pl.multiple_of((block & 255) * 128, 128), 128)]
            tiles.append(jnp.where((block >> 8) == blk, tile, jnp.zeros_like(tile)))
        out_ref[c] = jnp.concatenate(tiles, axis=1)


def merge_body(in_ref, out_ref):
    total = in_ref[0].astype(jnp.float32)
    for s in range(1, 16):
        total += in_ref[s].astype(jnp.float32)
    part = total.astype(jnp.bfloat16)
    for s in range(64):
        out_ref[s] = part


def row_tiles(p):
    return 2 * (p ^ 4), 2 * (p ^ 4) + 1


def first_body(tiles_ref, after_ref, held_ref, sems):
    def fetch(t):
        span = pl.ds(t * 5, 5)
        return pltpu.make_async_copy(tiles_ref.at[span], held_ref.at[span], sems.at[t])

    for t in range(GROUP):
        fetch(t).start()
    for t in range(GROUP):
        fetch(t).wait()


def product_body(
    irrep_ref, mine_ref, other_ref, first_ref, tiles_ref, out_ref, level_ref, held, slab, prod, code, in_sems, out_sems
):
    def fetch(t):
        return pltpu.make_async_copy(
            tiles_ref.at[pl.ds(t * 5, 5)], held.at[pl.ds((t - GROUP) * 5, 5)], in_sems.at[t - GROUP]
        )

    def store(t):
        return pltpu.make_async_copy(code.at[t], out_ref.at[t], out_sems.at[t])

    for t in range(GROUP, 16):
        fetch(t).start()
    core = lax.axis_index("pair") % 2
    for source, shift in ((mine_ref, core), (other_ref, 1 - core)):
        for c in range(16):
            for x in range(4):
                rows = pl.ds(pl.multiple_of((2 * x + shift) * 16, 16), 16)
                slab[c // 2, rows, (c % 2) * 256 : (c % 2) * 256 + 256] = source[c * 4 + x]

    count = GROUP * 5

    def multiply(step, source, offset, top):
        values = []
        for k in range(count + 1):
            if k < count:
                left = slab[jnp.maximum(irrep_ref[step * count + k], 0)]
                right = source[offset + k].reshape(512, 128)
                values.append(jnp.dot(left, right, preferred_element_type=jnp.float32))
            if k > 0:
                slot = step * count + k - 1
                value = values[k - 1]
                prod[slot] = value
                high = jnp.max(jnp.abs(value).reshape(16, 8, 128), axis=0)
                top = jnp.maximum(top, jnp.where(irrep_ref[slot] >= 0, high, 0.0))
        return top

    def later(step, top):
        for t in range(GROUP):
            fetch(step * GROUP + t).wait()
        return multiply(step, held, (step - 1) * count, top)

    top = multiply(0, first_ref, 0, jnp.zeros((8, 128), jnp.float32))
    top = lax.fori_loop(1, 16 // GROUP, later, top)
    top = jnp.max(jnp.max(top, axis=1, keepdims=True), axis=0, keepdims=True)
    level = jnp.ceil(jnp.log(jnp.maximum(top, 1e-30)) * (STEPS / LN2))
    level = jnp.broadcast_to(level, (8, 128))
    level_ref[...] = level.astype(jnp.int32)
    inverse = jnp.exp(level * (-LN2 / STEPS)) * TOP

    def quantise(t, carry):
        for k in range(5):
            value = prod[t * 5 + k]
            words = []
            for p in range(8):
                high, low = (
                    jnp.floor(value[u * 8 : u * 8 + 8, :] * inverse + 0.5).astype(jnp.int32) for u in row_tiles(p)
                )
                words.append((high << 16) | (low & 0xFFFF))
            for p in range(8):
                code[t, p, k] = words[p]
        store(t).start()
        return carry

    lax.fori_loop(0, 16, quantise, 0)
    for t in range(16):
        store(t).wait()


def select_body(from_ref, in_ref, level_ref, out_ref, words_ref, picked, sems, word_sems):
    def store(c):
        span = pl.ds(c * 2, 2)
        return pltpu.make_async_copy(picked.at[span], out_ref.at[span], sems.at[c])

    def store_words(c):
        span = pl.ds(c * 2, 2)
        return pltpu.make_async_copy(picked.at[span, pl.ds(0, 16)], words_ref.at[span], word_sems.at[c])

    def one(t, carry):
        for i in range(16):
            picked[t, i] = in_ref[from_ref[t * 16 + i]]
        picked[t, 16] = level_ref[...]
        return carry

    for c in range(8):
        lax.fori_loop(c * 2, c * 2 + 2, one, 0)
        store_words(c).start()
        store(c).start()
    for c in range(8):
        store_words(c).wait()
        store(c).wait()


def combine_body(own_ref, face_ref, here_ref, there_ref, pick_ref, sign_ref, out_ref, scale, result, sems):
    levels = jnp.concatenate([there_ref[s * 17 + 16] for s in range(16)], axis=0)
    pick = pick_ref[...]
    upper = jnp.dot(pick, (levels >> 5).astype(jnp.bfloat16), preferred_element_type=jnp.float32)
    lower = jnp.dot(pick, (levels & 31).astype(jnp.bfloat16), preferred_element_type=jnp.float32)
    value = jnp.exp((upper * 32.0 + lower) * (LN2 / STEPS)) * (1.0 / TOP)
    scale[:256] = value[:256]
    scale[256:] = value[256:] * sign_ref[...]

    def store(c):
        span = pl.ds(c * 4096, 4096)
        return pltpu.make_async_copy(result.at[:, span], out_ref.at[:, span], sems.at[c])

    def parts(word):
        return (word >> 16).astype(jnp.float32), ((word << 16) >> 16).astype(jnp.float32)

    def one(step, carry):
        rows = pl.multiple_of(step * 8, 8)
        own_scale = scale[pl.ds(rows, 8), :]
        face_scale = scale[pl.ds(256 + rows, 8), :]
        values = []
        for i in range(8):
            own = parts(here_ref[own_ref[step * 8 + i]])
            face = parts(there_ref[face_ref[step * 8 + i]])
            halves = [o * own_scale[i : i + 1, :] + f * face_scale[i : i + 1, :] for o, f in zip(own, face)]
            values.append(jnp.concatenate(halves, axis=0).astype(jnp.bfloat16))
        for i in range(8):
            result[:, pl.ds(pl.multiple_of((step * 8 + i) * 128, 128), 128)] = values[i]
        return carry

    for c in range(8):
        lax.fori_loop(c * 4, c * 4 + 4, one, 0)
        store(c).start()
    for c in range(8):
        store(c).wait()


def call_product(irreps, mine, other, first, tiles):
    dma = pltpu.SemaphoreType.DMA
    int32 = jnp.int32
    return call(
        product_body, [SMEM, VMEM, VMEM, VMEM, HBM], [HBM, VMEM],
        [pltpu.HBM((16, 8, 5, 8, 128), int32), jax.ShapeDtypeStruct((8, 128), int32)],
        [
            pltpu.VMEM((80 - GROUP * 5, 4, 128, 128), jnp.bfloat16),
            pltpu.VMEM((8, 128, 512), jnp.bfloat16),
            pltpu.VMEM((80, 128, 128), jnp.float32),
            pltpu.VMEM((16, 8, 5, 8, 128), int32),
            dma((16 - GROUP,)),
            dma((16,)),
        ],
        48 * MIB, 1_342_177_280, 14 << 20,
    )(irreps, mine, other, first, tiles)


def call_first(tiles, after):
    shape = pltpu.VMEM((GROUP * 5, 4, 128, 128), jnp.bfloat16)
    return call(first_body, [HBM, pl.BlockSpec(memory_space=pl.ANY)], VMEM, shape, [pltpu.SemaphoreType.DMA((GROUP,))], 47 * MIB, 0, 5 << 20)(tiles, after)


def call_combine(own, face, here, there, pick, signs):
    scratch = [
        pltpu.VMEM((512, 128), jnp.float32),
        pltpu.VMEM((16, 32768), jnp.bfloat16),
        pltpu.SemaphoreType.DMA((8,)),
    ]
    out = jax.ShapeDtypeStruct((16, 32768), jnp.bfloat16)
    return call(combine_body, [SMEM] * 2 + [VMEM] * 4, HBM, out, scratch, 16 * MIB, 0, 4 << 20)(
        own, face, here, there, pick, signs
    )


def swap(value, mask):
    return lax.ppermute(value, "pair", [(i, i ^ mask) for i in range(8)])


def local(amplitudes, integrals, block_irrep, slab_blocks, owner, partner, sign):
    blk = lax.axis_index("blk")
    pair = lax.axis_index("pair")
    me = blk * 8 + pair
    int32 = jnp.int32
    dma = pltpu.SemaphoreType.DMA

    parts = call(
        extract_body, [SMEM, VMEM], VMEM, jax.ShapeDtypeStruct((16, 16, 256), jnp.bfloat16), [], 53 * MIB, 0, 1 << 20
    )(slab_blocks, amplitudes)
    parts = lax.all_to_all(parts, "blk", split_axis=0, concat_axis=0, tiled=True)
    copies = call(
        merge_body, [VMEM], VMEM, jax.ShapeDtypeStruct((64, 16, 256), jnp.bfloat16), [], 4 * MIB, 0, 1 << 20
    )(parts)
    groups = [[c + 2 * i for i in range(64)] for c in range(2)]
    mine = lax.all_to_all(copies, BOTH, split_axis=0, concat_axis=0, tiled=True, axis_index_groups=groups)
    other = swap(mine, 1)

    ids = jnp.arange(256, dtype=int32)
    stored = (owner == me).reshape(16, 256)
    earlier = (ids[:, None] < ids[None, :]).astype(jnp.bfloat16)
    slot_rank = jnp.dot(stored.astype(jnp.bfloat16), earlier, preferred_element_type=jnp.float32).astype(int32)
    labels = block_irrep.reshape(16, 256) + 1
    chosen = stored[:, None, :] & (slot_rank[:, None, :] == jnp.arange(5, dtype=int32)[None, :, None])
    slot_irrep = (jnp.sum(jnp.where(chosen, labels[:, None, :], 0), axis=2) - 1).reshape(80)

    my_owner = lax.dynamic_slice_in_dim(owner, blk * 256, 256)
    my_partner = lax.dynamic_slice_in_dim(partner, blk * 256, 256)
    my_sign = lax.dynamic_slice_in_dim(sign, blk * 256, 256)
    before = ids[None, :] < ids[:, None]
    rank = jnp.sum((my_owner[None, :] == my_owner[:, None]) & before, axis=1).astype(int32)
    arrive = my_owner * 5 + rank
    leave_key = (my_partner // 256) * 256 + ids
    leave = jnp.sum(leave_key[None, :] < leave_key[:, None], axis=1).astype(int32)
    leaving = jnp.sum(jnp.where(leave[None, :] == ids[:, None], arrive[None, :], 0), axis=1).astype(int32)
    back = jnp.sum(my_partner[None, :] < my_partner[:, None], axis=1).astype(int32)
    all_ids = jnp.arange(4096, dtype=int32)
    face_owner = jnp.sum(jnp.where(my_partner[:, None] == all_ids[None, :], owner[None, :], 0), axis=1)
    back = back + back // 16
    rows = jnp.concatenate([my_owner ^ pair, face_owner ^ pair])
    pick = (rows[:, None] == jnp.arange(128, dtype=int32)[None, :]).astype(jnp.bfloat16)
    signs = jnp.broadcast_to(my_sign.astype(jnp.float32)[:, None], (256, 128))

    first = call_first(integrals, mine)
    coded, level = call_product(slot_irrep, mine, other, first, integrals)
    arrived = lax.all_to_all(coded.reshape(128, 40, 128), BOTH, split_axis=0, concat_axis=0, tiled=True)
    arrived = arrived.reshape(640, 8, 128)
    levels = level[:1]
    for mask in (1, 2, 4):
        levels = jnp.concatenate([levels, swap(levels, mask)], axis=0)
    outgoing, words = call(
        select_body, [SMEM, VMEM, VMEM], [HBM, HBM],
        [pltpu.HBM((16, 17, 8, 128), int32), pltpu.HBM((16, 16, 8, 128), int32)],
        [pltpu.VMEM((16, 17, 8, 128), int32), dma((8,)), dma((8,))], 16 * MIB, 0, 4 << 20,
    )(leaving, arrived, levels)
    own = swap(words, 4).reshape(256, 8, 128)
    incoming = lax.all_to_all(outgoing, "blk", split_axis=0, concat_axis=0, tiled=True).reshape(272, 8, 128)
    return call_combine(leave, back, own, incoming, pick, signs)


def solution(mesh):
    placed = (P("pair", "blk"), P(BOTH, None, None, None), P(), P(), P(), P(), P())
    return jax.shard_map(local, mesh=mesh, in_specs=placed, out_specs=P("pair", "blk"), check_vma=False)
```

```python
import jax
import jax.numpy as jnp
from jax import lax
from jax.experimental import pallas as pl
from jax.experimental.pallas import tpu as pltpu
from jax.sharding import PartitionSpec as P

BOTH = ("blk", "pair")
TOP = 32760.0
STEPS = 64.0
LN2 = 0.6931471805599453
MIB = 1 << 20
GROUP = 4
VMEM = pl.BlockSpec(memory_space=pltpu.VMEM)
HBM = pl.BlockSpec(memory_space=pltpu.HBM)
SMEM = pl.BlockSpec(memory_space=pltpu.SMEM)


def call(body, ins, outs, shapes, scratch, vmem, flops, moved):
    return pl.pallas_call(
        body,
        in_specs=ins,
        out_specs=outs,
        out_shape=shapes,
        scratch_shapes=scratch,
        compiler_params=pltpu.CompilerParams(vmem_limit_bytes=vmem),
        cost_estimate=pl.CostEstimate(flops=flops, bytes_accessed=moved, transcendentals=0),
    )


def extract_body(blocks_ref, amp_ref, out_ref):
    blk = lax.axis_index("blk")
    for c in range(16):
        tiles = []
        for n in (2 * c, 2 * c + 1):
            block = blocks_ref[n]
            tile = amp_ref[:, pl.ds(pl.multiple_of((block & 255) * 128, 128), 128)]
            tiles.append(jnp.where((block >> 8) == blk, tile, jnp.zeros_like(tile)))
        out_ref[c] = jnp.concatenate(tiles, axis=1)


def merge_body(in_ref, out_ref):
    total = in_ref[0].astype(jnp.float32)
    for s in range(1, 16):
        total += in_ref[s].astype(jnp.float32)
    part = total.astype(jnp.bfloat16)
    for s in range(64):
        out_ref[s] = part


def row_tiles(p):
    return 2 * (p ^ 4), 2 * (p ^ 4) + 1


def first_body(tiles_ref, after_ref, held_ref, sems):
    def fetch(t):
        span = pl.ds(t * 5, 5)
        return pltpu.make_async_copy(tiles_ref.at[span], held_ref.at[span], sems.at[t])

    for t in range(GROUP):
        fetch(t).start()
    for t in range(GROUP):
        fetch(t).wait()


def product_body(
    irrep_ref, mine_ref, other_ref, first_ref, tiles_ref, out_ref, level_ref, held, slab, prod, code, in_sems, out_sems
):
    def fetch(t):
        return pltpu.make_async_copy(
            tiles_ref.at[pl.ds(t * 5, 5)], held.at[pl.ds((t - GROUP) * 5, 5)], in_sems.at[t - GROUP]
        )

    def store(t):
        return pltpu.make_async_copy(code.at[t], out_ref.at[t], out_sems.at[t])

    for t in range(GROUP, 16):
        fetch(t).start()
    core = lax.axis_index("pair") % 2
    for source, shift in ((mine_ref, core), (other_ref, 1 - core)):
        for c in range(16):
            for x in range(4):
                rows = pl.ds(pl.multiple_of((2 * x + shift) * 16, 16), 16)
                slab[c // 2, rows, (c % 2) * 256 : (c % 2) * 256 + 256] = source[c * 4 + x]

    count = GROUP * 5

    def multiply(step, source, offset, top):
        values = []
        for k in range(count + 1):
            if k < count:
                left = slab[jnp.maximum(irrep_ref[step * count + k], 0)]
                right = source[offset + k].reshape(512, 128)
                values.append(jnp.dot(left, right, preferred_element_type=jnp.float32))
            if k > 0:
                slot = step * count + k - 1
                value = values[k - 1]
                prod[slot] = value
                high = jnp.max(jnp.abs(value).reshape(16, 8, 128), axis=0)
                top = jnp.maximum(top, jnp.where(irrep_ref[slot] >= 0, high, 0.0))
        return top

    def later(step, top):
        for t in range(GROUP):
            fetch(step * GROUP + t).wait()
        return multiply(step, held, (step - 1) * count, top)

    top = multiply(0, first_ref, 0, jnp.zeros((8, 128), jnp.float32))
    top = lax.fori_loop(1, 16 // GROUP, later, top)
    top = jnp.max(jnp.max(top, axis=1, keepdims=True), axis=0, keepdims=True)
    level = jnp.ceil(jnp.log(jnp.maximum(top, 1e-30)) * (STEPS / LN2))
    level = jnp.broadcast_to(level, (8, 128))
    level_ref[...] = level.astype(jnp.int32)
    inverse = jnp.exp(level * (-LN2 / STEPS)) * TOP

    def quantise(t, carry):
        for k in range(5):
            value = prod[t * 5 + k]
            words = []
            for p in range(8):
                high, low = (
                    jnp.floor(value[u * 8 : u * 8 + 8, :] * inverse + 0.5).astype(jnp.int32) for u in row_tiles(p)
                )
                words.append((high << 16) | (low & 0xFFFF))
            for p in range(8):
                code[t, p, k] = words[p]
        store(t).start()
        return carry

    lax.fori_loop(0, 16, quantise, 0)
    for t in range(16):
        store(t).wait()


def select_body(from_ref, in_ref, level_ref, out_ref, words_ref, picked, sems, word_sems):
    def store(c):
        span = pl.ds(c * 2, 2)
        return pltpu.make_async_copy(picked.at[span], out_ref.at[span], sems.at[c])

    def store_words(c):
        span = pl.ds(c * 2, 2)
        return pltpu.make_async_copy(picked.at[span, pl.ds(0, 16)], words_ref.at[span], word_sems.at[c])

    def one(t, carry):
        for i in range(16):
            picked[t, i] = in_ref[from_ref[t * 16 + i]]
        picked[t, 16] = level_ref[...]
        return carry

    for c in range(8):
        lax.fori_loop(c * 2, c * 2 + 2, one, 0, unroll=2)
        store_words(c).start()
        store(c).start()
    for c in range(8):
        store_words(c).wait()
        store(c).wait()


def combine_body(own_ref, face_ref, here_ref, there_ref, pick_ref, sign_ref, out_ref, scale, result, sems):
    levels = jnp.concatenate([there_ref[s * 17 + 16] for s in range(16)], axis=0)
    pick = pick_ref[...]
    upper = jnp.dot(pick, (levels >> 5).astype(jnp.bfloat16), preferred_element_type=jnp.float32)
    lower = jnp.dot(pick, (levels & 31).astype(jnp.bfloat16), preferred_element_type=jnp.float32)
    value = jnp.exp((upper * 32.0 + lower) * (LN2 / STEPS)) * (1.0 / TOP)
    scale[:256] = value[:256]
    scale[256:] = value[256:] * sign_ref[...]

    def store(c):
        span = pl.ds(c * 4096, 4096)
        return pltpu.make_async_copy(result.at[:, span], out_ref.at[:, span], sems.at[c])

    def parts(word):
        return (word >> 16).astype(jnp.float32), ((word << 16) >> 16).astype(jnp.float32)

    def one(step, carry):
        rows = pl.multiple_of(step * 8, 8)
        own_scale = scale[pl.ds(rows, 8), :]
        face_scale = scale[pl.ds(256 + rows, 8), :]
        values = []
        for i in range(8):
            own = parts(here_ref[own_ref[step * 8 + i]])
            face = parts(there_ref[face_ref[step * 8 + i]])
            halves = [o * own_scale[i : i + 1, :] + f * face_scale[i : i + 1, :] for o, f in zip(own, face)]
            values.append(jnp.concatenate(halves, axis=0).astype(jnp.bfloat16))
        for i in range(8):
            result[:, pl.ds(pl.multiple_of((step * 8 + i) * 128, 128), 128)] = values[i]
        return carry

    for c in range(8):
        lax.fori_loop(c * 4, c * 4 + 4, one, 0, unroll=4)
        store(c).start()
    for c in range(8):
        store(c).wait()


def call_product(irreps, mine, other, first, tiles):
    dma = pltpu.SemaphoreType.DMA
    int32 = jnp.int32
    return call(
        product_body, [SMEM, VMEM, VMEM, VMEM, HBM], [HBM, VMEM],
        [pltpu.HBM((16, 8, 5, 8, 128), int32), jax.ShapeDtypeStruct((8, 128), int32)],
        [
            pltpu.VMEM((80 - GROUP * 5, 4, 128, 128), jnp.bfloat16),
            pltpu.VMEM((8, 128, 512), jnp.bfloat16),
            pltpu.VMEM((80, 128, 128), jnp.float32),
            pltpu.VMEM((16, 8, 5, 8, 128), int32),
            dma((16 - GROUP,)),
            dma((16,)),
        ],
        48 * MIB, 1_342_177_280, 14 << 20,
    )(irreps, mine, other, first, tiles)


def call_first(tiles, after):
    shape = pltpu.VMEM((GROUP * 5, 4, 128, 128), jnp.bfloat16)
    return call(first_body, [HBM, pl.BlockSpec(memory_space=pl.ANY)], VMEM, shape, [pltpu.SemaphoreType.DMA((GROUP,))], 47 * MIB, 0, 5 << 20)(tiles, after)


def call_combine(own, face, here, there, pick, signs):
    scratch = [
        pltpu.VMEM((512, 128), jnp.float32),
        pltpu.VMEM((16, 32768), jnp.bfloat16),
        pltpu.SemaphoreType.DMA((8,)),
    ]
    out = jax.ShapeDtypeStruct((16, 32768), jnp.bfloat16)
    return call(combine_body, [SMEM] * 2 + [VMEM] * 4, HBM, out, scratch, 16 * MIB, 0, 4 << 20)(
        own, face, here, there, pick, signs
    )


def swap(value, mask):
    return lax.ppermute(value, "pair", [(i, i ^ mask) for i in range(8)])


def local(amplitudes, integrals, block_irrep, slab_blocks, owner, partner, sign):
    blk = lax.axis_index("blk")
    pair = lax.axis_index("pair")
    me = blk * 8 + pair
    int32 = jnp.int32
    dma = pltpu.SemaphoreType.DMA

    parts = call(
        extract_body, [SMEM, VMEM], VMEM, jax.ShapeDtypeStruct((16, 16, 256), jnp.bfloat16), [], 53 * MIB, 0, 1 << 20
    )(slab_blocks, amplitudes)
    parts = lax.all_to_all(parts, "blk", split_axis=0, concat_axis=0, tiled=True)
    copies = call(
        merge_body, [VMEM], VMEM, jax.ShapeDtypeStruct((64, 16, 256), jnp.bfloat16), [], 4 * MIB, 0, 1 << 20
    )(parts)
    groups = [[c + 2 * i for i in range(64)] for c in range(2)]
    mine = lax.all_to_all(copies, BOTH, split_axis=0, concat_axis=0, tiled=True, axis_index_groups=groups)
    other = swap(mine, 1)

    ids = jnp.arange(256, dtype=int32)
    stored = (owner == me).reshape(16, 256)
    earlier = (ids[:, None] < ids[None, :]).astype(jnp.bfloat16)
    slot_rank = jnp.dot(stored.astype(jnp.bfloat16), earlier, preferred_element_type=jnp.float32).astype(int32)
    labels = block_irrep.reshape(16, 256) + 1
    chosen = stored[:, None, :] & (slot_rank[:, None, :] == jnp.arange(5, dtype=int32)[None, :, None])
    slot_irrep = (jnp.sum(jnp.where(chosen, labels[:, None, :], 0), axis=2) - 1).reshape(80)

    my_owner = lax.dynamic_slice_in_dim(owner, blk * 256, 256)
    my_partner = lax.dynamic_slice_in_dim(partner, blk * 256, 256)
    my_sign = lax.dynamic_slice_in_dim(sign, blk * 256, 256)
    before = ids[None, :] < ids[:, None]
    rank = jnp.sum((my_owner[None, :] == my_owner[:, None]) & before, axis=1).astype(int32)
    arrive = my_owner * 5 + rank
    leave_key = (my_partner // 256) * 256 + ids
    leave = jnp.sum(leave_key[None, :] < leave_key[:, None], axis=1).astype(int32)
    leaving = jnp.sum(jnp.where(leave[None, :] == ids[:, None], arrive[None, :], 0), axis=1).astype(int32)
    back = jnp.sum(my_partner[None, :] < my_partner[:, None], axis=1).astype(int32)
    all_ids = jnp.arange(4096, dtype=int32)
    face_owner = jnp.sum(jnp.where(my_partner[:, None] == all_ids[None, :], owner[None, :], 0), axis=1)
    back = back + back // 16
    rows = jnp.concatenate([my_owner ^ pair, face_owner ^ pair])
    pick = (rows[:, None] == jnp.arange(128, dtype=int32)[None, :]).astype(jnp.bfloat16)
    signs = jnp.broadcast_to(my_sign.astype(jnp.float32)[:, None], (256, 128))

    first = call_first(integrals, mine)
    coded, level = call_product(slot_irrep, mine, other, first, integrals)
    arrived = lax.all_to_all(coded.reshape(128, 40, 128), BOTH, split_axis=0, concat_axis=0, tiled=True)
    arrived = arrived.reshape(640, 8, 128)
    levels = level[:1]
    for mask in (1, 2, 4):
        levels = jnp.concatenate([levels, swap(levels, mask)], axis=0)
    outgoing, words = call(
        select_body, [SMEM, VMEM, VMEM], [HBM, HBM],
        [pltpu.HBM((16, 17, 8, 128), int32), pltpu.HBM((16, 16, 8, 128), int32)],
        [pltpu.VMEM((16, 17, 8, 128), int32), dma((8,)), dma((8,))], 16 * MIB, 0, 4 << 20,
    )(leaving, arrived, levels)
    own = swap(words, 4).reshape(256, 8, 128)
    incoming = lax.all_to_all(outgoing, "blk", split_axis=0, concat_axis=0, tiled=True).reshape(272, 8, 128)
    return call_combine(leave, back, own, incoming, pick, signs)


def solution(mesh):
    placed = (P("pair", "blk"), P(BOTH, None, None, None), P(), P(), P(), P(), P())
    return jax.shard_map(local, mesh=mesh, in_specs=placed, out_specs=P("pair", "blk"), check_vma=False)
```
